128 devices in a mesh: ctx: 32 (over y_lo, z, x), head: 4 (over y_hi, core).
Axes of the slice: x: 4, y: 4 (y_hi: 2, y_lo: 2; y = y_hi * 2 + y_lo), z: 4, core: 2. Of those that a mesh axis runs over, the one named last changes fastest.
Arguments:
- query_raw: bfloat16 [32768, 4096], P('ctx', 'head')
- key_raw: bfloat16 [32768, 1024], P('ctx', 'head')
- values: bfloat16 [32768, 1024], P('ctx', 'head'), may hold values from -6 to 6
- output_gradient: bfloat16 [32768, 4096], P('ctx', 'head'), may hold values from -6 to 6
- query_gain: float32 [4096], P('head'), may hold values from 0.5 to 3
- key_norm_gain: float32 [1024], P('head'), may hold values from 0.5 to 3
- block_docs: int32 [256], replicated, may hold values from 0 to 41, never falling along the last dimension, each value on 1 to 24 neighbouring positions
Outputs:
- attended: bfloat16 [32768, 4096], P('ctx', 'head')
- query_grad: bfloat16 [32768, 4096], P('ctx', 'head')
- key_raw_gradient: bfloat16 [32768, 1024], P('ctx', 'head')
- value_grad: bfloat16 [32768, 1024], P('ctx', 'head')
- query_gain_grad: float32 [4096], P('head')
- key_gain_grad: float32 [1024], P('head')
The draws below stay inside these ranges and needn't reach their ends.
Inputs may be any that keep to these rules, and one draw needn't show every extreme that they name: `block_docs`: document numbers never fall from one block to the next; each document covers 1 to 24 consecutive mask blocks, and one covers exactly 24.
All inputs are finite; a program needn't handle non-finite values.
Results may differ from the reference program's by a relative error of at most 0.024.
The reference program's roundings to bfloat16 on the way count: a program that leaves them out, or rounds other values in their place, can miss the bound.
Values may be sent and summed in bfloat16 or wider, within the bound.
A program may use at most 128 MiB of HBM per device.

```python
import math
import jax
import jax.numpy as jnp
import numpy as np
from jax import lax

QUERY_HEADS = 32
KEY_VALUE_HEADS = 8
HEAD_SIZE = 128
WINDOW_REACH = 512
BLOCK = 128
MOST = 24
SEQUENCE_TOKENS = 32768
BLOCKS = 256
DOCS = 42


def qk_fields(key):
    pieces = jax.random.split(jax.random.fold_in(key, 41), 5)
    query_width = QUERY_HEADS * HEAD_SIZE
    key_span_width = KEY_VALUE_HEADS * HEAD_SIZE
    col_rise = 3.0
    row_top = 10.0
    query_base = jax.random.normal(pieces[0], (SEQUENCE_TOKENS, query_width), jnp.float32)
    key_base = jax.random.normal(pieces[1], (SEQUENCE_TOKENS, key_span_width), jnp.float32)
    row_scale = jnp.exp(jax.random.uniform(pieces[2], (SEQUENCE_TOKENS, 1), jnp.float32) * math.log(row_top))
    query_cols = jnp.exp(jnp.arange(query_width, dtype=jnp.float32) / (query_width - 1) * math.log(col_rise) + jax.random.uniform(pieces[3], (query_width,), jnp.float32) * math.log(10.0))
    key_cols = jnp.exp(jnp.arange(key_span_width, dtype=jnp.float32) / (key_span_width - 1) * math.log(col_rise) + jax.random.uniform(pieces[4], (key_span_width,), jnp.float32) * math.log(10.0))
    query = query_base * row_scale * query_cols
    keyfield = key_base * row_scale * key_cols
    return (query, keyfield)


def draw_query_raw(key, part):
    return qk_fields(key)[0].astype(jnp.bfloat16)


def draw_key_raw(key, part):
    return qk_fields(key)[1].astype(jnp.bfloat16)


def shard_levels(own_key, shape, cuts, smallest, top_value):
    level = 1.0
    for dim, shards_of in cuts:
        steps = jax.random.uniform(jax.random.fold_in(jax.random.fold_in(own_key, 6), dim), (shards_of,), jnp.float32, smallest / len(cuts), top_value / len(cuts))
        level = level * jnp.repeat(jnp.exp(steps), shape[dim] // shards_of).reshape((-1,) + (1,) * (len(shape) - 1 - dim))
    return level


def split_up(number_of, total, bound, skew):
    portions = [(1 << 20) // math.isqrt(standing ** skew) + 1 for standing in range(2, number_of + 1)]
    spare, holding = total - bound - (number_of - 1), [1] * (number_of - 1)
    while spare > 0:
        movable = [i for i in range(number_of - 1) if holding[i] < bound]
        mass, remaining = sum([portions[i] for i in movable]), spare
        for i in movable:
            addition = min(bound - holding[i], max(1, remaining * portions[i] // mass), spare)
            holding[i] = holding[i] + addition
            spare = spare - addition
    return np.array([bound] + holding)


def ragged_sizes(rng, count, total, most, slope):
    if count == 2:
        one = jax.random.randint(rng, (), max(1, total - most), min(most, total - 1) + 1)
        return jnp.stack([one, total - one])
    lengths = jnp.asarray(split_up(count, total, most, slope), jnp.int32)
    pairs = (count - 1) // 2
    source_of, receiver = lengths[1:1 + 2 * pairs:2], lengths[2:2 + 2 * pairs:2]
    slack = jnp.minimum(source_of - 1, most - receiver)
    passed = jax.random.randint(jax.random.fold_in(rng, 1), (pairs,), 0, 1 << 20) % (slack + 1)
    lengths = lengths.at[1:1 + 2 * pairs:2].set(source_of - passed).at[2:2 + 2 * pairs:2].set(receiver + passed)
    return lengths[jax.random.permutation(jax.random.fold_in(rng, 2), count)]


def normal_values(key, shape, width, most, cuts=(), kind=jnp.bfloat16):
    values = width * jax.random.normal(key, shape, jnp.float32)
    if cuts:
        values = values * shard_levels(key, shape, cuts, -0.22, 0.18)
    return jnp.clip(values, -most, most).astype(kind)


def setup_inputs(seed: int = 0) -> dict:
    seeds = jax.random.split(jax.random.key(seed), 8)
    query_raw = draw_query_raw(jax.random.fold_in(seeds[7], 71), 0)
    key_raw = draw_key_raw(jax.random.fold_in(seeds[7], 71), 0)
    values = normal_values(seeds[2], (SEQUENCE_TOKENS, KEY_VALUE_HEADS * HEAD_SIZE), 1.0, 6.0, ((0, 32), (1, 4)))
    output_gradient = normal_values(seeds[3], (SEQUENCE_TOKENS, QUERY_HEADS * HEAD_SIZE), 1.0, 6.0, ((0, 32), (1, 4)))
    query_gain = jnp.clip(0.5 + 2.5 * jax.random.uniform(seeds[4], (QUERY_HEADS * HEAD_SIZE,), jnp.float32) ** shard_levels(seeds[4], (QUERY_HEADS * HEAD_SIZE,), ((0, 4),), -0.2, 0.2), 0.5, 3.0)
    key_norm_gain = jnp.clip(0.5 + 2.5 * jax.random.uniform(seeds[5], (KEY_VALUE_HEADS * HEAD_SIZE,), jnp.float32) ** shard_levels(seeds[5], (KEY_VALUE_HEADS * HEAD_SIZE,), ((0, 4),), -0.2, 0.2), 0.5, 3.0)
    block_docs = jnp.searchsorted(jnp.cumsum(ragged_sizes(seeds[6], DOCS, BLOCKS, MOST, 2)), jnp.arange(BLOCKS), side="right").astype(jnp.int32)
    return {"query_raw": query_raw, "key_raw": key_raw, "values": values, "output_gradient": output_gradient, "query_gain": query_gain, "key_norm_gain": key_norm_gain, "block_docs": block_docs}


EPS = 1e-06
NEGATIVE = -1e+30

def rounded(tensor):
    return lax.optimization_barrier(tensor.astype(jnp.bfloat16)).astype(jnp.float32)

def rescale_each_row(raw, gain):
    floats = raw.astype(jnp.float32)
    scale_rows = lax.rsqrt(lax.optimization_barrier(jnp.mean(floats * floats, axis=1, keepdims=True)) + EPS)
    unit_rows = floats * scale_rows
    return (scale_rows, unit_rows, (unit_rows * gain).astype(jnp.bfloat16))

def norm_backward(grad, unit_rows, scale_rows, gain):
    scaled = grad * gain
    inner = lax.optimization_barrier(jnp.mean(scaled * unit_rows, axis=1, keepdims=True))
    return (scale_rows * (scaled - unit_rows * inner)).astype(jnp.bfloat16)

def reference(query_raw, key_raw, values, output_gradient, query_gain, key_norm_gain, block_docs):
    query_group_count = QUERY_HEADS // KEY_VALUE_HEADS
    stride_rows = min(512, WINDOW_REACH)
    softmax_scale = HEAD_SIZE ** (-0.5)
    query_scale, query_unit, query_normalized = rescale_each_row(query_raw, query_gain)
    key_inverse_scale, key_unit_rows, key_normalized = rescale_each_row(key_raw, key_norm_gain)
    key_padded = jnp.concatenate([jnp.zeros((WINDOW_REACH, KEY_VALUE_HEADS * HEAD_SIZE), jnp.bfloat16), key_normalized])
    value_padded = jnp.concatenate([jnp.zeros((WINDOW_REACH, KEY_VALUE_HEADS * HEAD_SIZE), jnp.bfloat16), values])
    doc_rows = jnp.repeat(block_docs, BLOCK)
    doc_pad = jnp.concatenate([jnp.full((WINDOW_REACH,), -1, jnp.int32), doc_rows])
    distance = jnp.arange(stride_rows, dtype=jnp.int32)[:, None] + WINDOW_REACH - jnp.arange(stride_rows + WINDOW_REACH, dtype=jnp.int32)[None, :]

    def attend(running, block_index):
        key_gradient_total, value_gradient_total = running
        leading_row = (block_index * stride_rows).astype(jnp.int32)
        key_total_count = stride_rows + WINDOW_REACH
        query_block = lax.dynamic_slice_in_dim(query_normalized, leading_row, stride_rows, 0).astype(jnp.float32).reshape(stride_rows, KEY_VALUE_HEADS, query_group_count, HEAD_SIZE)
        gradient_block = lax.dynamic_slice_in_dim(output_gradient, leading_row, stride_rows, 0).astype(jnp.float32).reshape(stride_rows, KEY_VALUE_HEADS, query_group_count, HEAD_SIZE)
        key_block = lax.dynamic_slice_in_dim(key_padded, leading_row, key_total_count, 0).astype(jnp.float32).reshape(key_total_count, KEY_VALUE_HEADS, HEAD_SIZE)
        value_block = lax.dynamic_slice_in_dim(value_padded, leading_row, key_total_count, 0).astype(jnp.float32).reshape(key_total_count, KEY_VALUE_HEADS, HEAD_SIZE)
        doc_query = lax.dynamic_slice_in_dim(doc_rows, leading_row, stride_rows, 0)
        doc_keys = lax.dynamic_slice_in_dim(doc_pad, leading_row, key_total_count, 0)
        visible = (distance >= 0) & (distance < WINDOW_REACH) & (doc_query[:, None] == doc_keys[None, :])
        scores = jnp.einsum('ighd,jgd->ghij', query_block, key_block) * softmax_scale
        row_max = lax.optimization_barrier(jnp.max(jnp.where(visible, scores, NEGATIVE), axis=-1, keepdims=True))
        expo = jnp.where(visible, jnp.exp(scores - row_max), 0.0)
        weights = expo / lax.optimization_barrier(jnp.sum(expo, axis=-1, keepdims=True))
        weights_low = rounded(weights)
        out_blk = jnp.einsum('ghij,jgd->ighd', weights_low, value_block).astype(jnp.bfloat16)
        delta = jnp.einsum('ighd,ighd->ghi', gradient_block, out_blk.astype(jnp.float32))
        dweights = jnp.einsum('ighd,jgd->ghij', gradient_block, value_block)
        dscores_low = rounded(weights * (dweights - delta[..., None]))
        dquery_blk = jnp.einsum('ghij,jgd->ighd', dscores_low, key_block) * softmax_scale
        key_gradient_block = jnp.einsum('ghij,ighd->jgd', dscores_low, query_block) * softmax_scale
        value_gradient_block = jnp.einsum('ghij,ighd->jgd', weights_low, gradient_block)
        present_key = lax.dynamic_slice_in_dim(key_gradient_total, leading_row, key_total_count, 0)
        key_gradient_total = lax.dynamic_update_slice_in_dim(key_gradient_total, present_key + key_gradient_block.reshape(key_total_count, KEY_VALUE_HEADS * HEAD_SIZE), leading_row, 0)
        present_value = lax.dynamic_slice_in_dim(value_gradient_total, leading_row, key_total_count, 0)
        value_gradient_total = lax.dynamic_update_slice_in_dim(value_gradient_total, present_value + value_gradient_block.reshape(key_total_count, KEY_VALUE_HEADS * HEAD_SIZE), leading_row, 0)
        return ((key_gradient_total, value_gradient_total), (out_blk.reshape(stride_rows, QUERY_HEADS * HEAD_SIZE), dquery_blk.reshape(stride_rows, QUERY_HEADS * HEAD_SIZE)))
    blank_start = jnp.zeros((SEQUENCE_TOKENS + WINDOW_REACH, KEY_VALUE_HEADS * HEAD_SIZE), jnp.float32)
    (key_gradient_total, value_gradient_total), (out_blocks, dquery_blocks) = lax.scan(attend, (blank_start, blank_start), jnp.arange(SEQUENCE_TOKENS // stride_rows, dtype=jnp.int32))
    attended = out_blocks.reshape(SEQUENCE_TOKENS, QUERY_HEADS * HEAD_SIZE)
    dquery = dquery_blocks.reshape(SEQUENCE_TOKENS, QUERY_HEADS * HEAD_SIZE)
    dkey = key_gradient_total[WINDOW_REACH:]
    value_grad = value_gradient_total[WINDOW_REACH:].astype(jnp.bfloat16)
    query_grad = norm_backward(dquery, query_unit, query_scale, query_gain)
    key_raw_gradient = norm_backward(dkey, key_unit_rows, key_inverse_scale, key_norm_gain)
    query_gain_grad = lax.optimization_barrier(jnp.sum(dquery * query_unit, axis=0))
    key_gain_grad = lax.optimization_barrier(jnp.sum(dkey * key_unit_rows, axis=0))
    return (attended, query_grad, key_raw_gradient, value_grad, query_gain_grad, key_gain_grad)
```

```python
import jax
import jax.numpy as jnp
from jax import lax
from jax.experimental import pallas as pl
from jax.experimental.pallas import tpu as pltpu
from jax.sharding import PartitionSpec as P

QUERY_HEADS = 32
KEY_VALUE_HEADS = 8
HEAD_SIZE = 128
WINDOW_REACH = 512
BLOCK = 128
EPS = 1e-06
NEGATIVE = -1e30
SCALE = HEAD_SIZE ** (-0.5)
SCALE_LOG2 = SCALE * 1.4426950408889634

F32 = jnp.float32
BF16 = jnp.bfloat16
MESH = pl.DeviceIdType.MESH

TOKENS = 1024
BLOCKS_HERE = TOKENS // BLOCK
HALO = WINDOW_REACH
HALO_BLOCKS = HALO // BLOCK
WINDOW_BLOCKS = HALO_BLOCKS + 1
WINDOW = WINDOW_BLOCKS * BLOCK
EXT = HALO + TOKENS
GROUPS = 2
GROUP = 4
HEADS = GROUPS * GROUP
QCOLS = HEADS * HEAD_SIZE
KCOLS = GROUPS * HEAD_SIZE
HEAD_PEERS = 4
GAIN_ROWS = 16


def dot(a, b, ca, cb):
    return lax.dot_general(a, b, (((ca,), (cb,)), ((), ())), preferred_element_type=F32)


def block_rows(b):
    return pl.ds(pl.multiple_of(b * BLOCK, BLOCK), BLOCK)


def cols(t):
    return slice(t * 128, (t + 1) * 128)


def column(row):
    return jnp.broadcast_to(row, (128, 128)).T


def row_sums(tile):
    return jnp.sum(tile.T, axis=0, keepdims=True)


def eight(tile):
    return jnp.sum(tile.reshape(16, 8, tile.shape[1]), axis=0)


def kernel(
    q_in, k_in, v_in, g_in, q_gain, k_gain, docs,
    att_out, qg_out, kg_out, vg_out, qgain_out, kgain_out,
    q_raw, go, att, qgrad, u_all, qn,
    k_raw, vals, kn, k_t, v_t, dk, dv,
    back_k, back_v, got_k, got_v, kgrad, vgrad,
    q_col, k_col, tri,
    stat, stat_all, k_stat, halo_stat,
    inner, inner_all, kin, kin_all, hin, hin_all, hin_sum, hin_got,
    q_acc, k_acc, gains, gains_x, gains_z, gains_y,
    load_sem, out_sem, halo_send, halo_recv, stat_send, stat_recv,
    inner_send, inner_recv, back_send, back_recv, kin_send, kin_recv,
    hin_send, hin_recv, gain_send, gain_recv,
):
    ctx = lax.axis_index("ctx")
    head = lax.axis_index("head")
    x = ctx % 4
    z = (ctx // 4) % 4
    y = ctx // 16
    nxt = (ctx + 1) % 32
    prv = (ctx + 31) % 32

    def at_x(r):
        return (y * 4 + z) * 4 + (x + r) % 4

    def at_z(r):
        return (y * 4 + (z + r) % 4) * 4 + x

    at_y = (((y + 1) % 2) * 4 + z) * 4 + x

    def at_head(r):
        return (head + r) % HEAD_PEERS

    def remote(src, dst, send, recv, **where):
        return pltpu.make_async_remote_copy(
            src_ref=src, dst_ref=dst, send_sem=send, recv_sem=recv,
            device_id=where, device_id_type=MESH,
        )

    barrier = pltpu.get_barrier_semaphore()
    for r in range(1, 4):
        pl.semaphore_signal(barrier, inc=1, device_id={"head": at_head(r)}, device_id_type=MESH)
        pl.semaphore_signal(barrier, inc=1, device_id={"ctx": at_x(r)}, device_id_type=MESH)
        pl.semaphore_signal(barrier, inc=1, device_id={"ctx": at_z(r)}, device_id_type=MESH)
    for other in (nxt, prv, at_y):
        pl.semaphore_signal(barrier, inc=1, device_id={"ctx": other}, device_id_type=MESH)

    own = pl.ds(HALO, TOKENS)
    load_k = pltpu.make_async_copy(k_in, k_raw.at[own], load_sem.at[0])
    load_q = pltpu.make_async_copy(q_in, q_raw, load_sem.at[1])
    load_v = pltpu.make_async_copy(v_in, vals.at[own], load_sem.at[2])
    load_g = pltpu.make_async_copy(g_in, go, load_sem.at[3])
    load_k.start()
    load_q.start()
    load_v.start()
    load_g.start()

    pl.semaphore_wait(barrier, 12)
    tail = pl.ds(TOKENS - HALO, HALO)
    front = pl.ds(0, HALO)
    halo_copies = [
        remote(k_in.at[tail], k_raw.at[front], halo_send.at[0], halo_recv.at[0], ctx=nxt),
        remote(v_in.at[tail], vals.at[front], halo_send.at[1], halo_recv.at[1], ctx=nxt),
    ]
    for copy in halo_copies:
        copy.start()

    load_k.wait()
    load_q.wait()

    def squares(b, _):
        rows = block_rows(b)
        total = None
        for t in range(HEADS):
            part = q_raw[rows, cols(t)].astype(F32)
            total = part * part if total is None else total + part * part
        stat[pl.ds(b, 1), :] = row_sums(total)
        total = None
        for t in range(GROUPS):
            part = k_raw[block_rows(b + HALO_BLOCKS), cols(t)].astype(F32)
            total = part * part if total is None else total + part * part
        stat[pl.ds(b + 8, 1), :] = row_sums(total)
        return 0

    lax.fori_loop(0, BLOCKS_HERE, squares, 0)
    stat_copies = [
        remote(stat, stat_all.at[head], stat_send.at[r - 1], stat_recv.at[r - 1], head=at_head(r))
        for r in range(1, 4)
    ]
    for copy in stat_copies:
        copy.start()
    stat_all[head] = stat[...]

    key_at = lax.broadcasted_iota(jnp.int32, (BLOCK, BLOCK), 0)
    query_at = lax.broadcasted_iota(jnp.int32, (BLOCK, BLOCK), 1)
    tri[0] = jnp.where(key_at > query_at, 0.0, NEGATIVE)
    tri[1] = jnp.where(key_at <= query_at, 0.0, NEGATIVE)
    dk[...] = jnp.zeros_like(dk)
    dv[...] = jnp.zeros_like(dv)
    q_acc[...] = jnp.zeros_like(q_acc)
    k_acc[...] = jnp.zeros_like(k_acc)
    load_v.wait()

    def turn_values(b, _):
        rows = block_rows(b)
        for t in range(GROUPS):
            v_t[cols(t), rows] = vals[rows, cols(t)].T
        return 0

    lax.fori_loop(HALO_BLOCKS, EXT // BLOCK, turn_values, 0)

    for copy in stat_copies:
        copy.wait_recv()
    total = stat_all[0] + stat_all[1] + stat_all[2] + stat_all[3]
    k_stat[...] = total[8:16]
    relay = remote(k_stat, halo_stat, halo_send.at[2], halo_recv.at[2], ctx=nxt)
    relay.start()

    q_scale = lax.rsqrt(total[0:8] / (QUERY_HEADS * HEAD_SIZE) + EPS)
    for b in range(BLOCKS_HERE):
        q_col[b * BLOCK : (b + 1) * BLOCK] = column(q_scale[b : b + 1])

    def norm_keys(b, scale_row):
        rows = slice(b * BLOCK, (b + 1) * BLOCK)
        scale = column(scale_row)
        k_col[rows] = scale
        for t in range(GROUPS):
            unit = k_raw[rows, cols(t)].astype(F32) * scale
            normed = (unit * k_gain[:, cols(t)]).astype(BF16)
            kn[rows, cols(t)] = normed
            k_t[cols(t), rows] = normed.T

    k_scale = lax.rsqrt(total[8:16] / (KEY_VALUE_HEADS * HEAD_SIZE) + EPS)
    for b in range(BLOCKS_HERE):
        norm_keys(b + HALO_BLOCKS, k_scale[b : b + 1])
    load_g.wait()

    def order(s):
        return jnp.where(s < 3, s + 4, jnp.where(s < 7, s - 3, 7))

    def att_copy(b):
        rows = block_rows(b)
        return pltpu.make_async_copy(att.at[rows], att_out.at[rows], out_sem.at[0, b])

    def qgrad_copy(b):
        rows = block_rows(b)
        return pltpu.make_async_copy(qgrad.at[rows], qg_out.at[rows], out_sem.at[1, b])

    def inner_copies(b):
        return [
            remote(
                inner.at[b], inner_all.at[head, b],
                inner_send.at[r - 1, b], inner_recv.at[r - 1, b], head=at_head(r),
            )
            for r in range(1, 4)
        ]

    def finish_queries(b):
        rows = block_rows(b)
        for copy in inner_copies(b):
            copy.wait_recv()
        summed = inner_all[0, b] + inner_all[1, b] + inner_all[2, b] + inner_all[3, b]
        mean = column(summed[0:1] / (QUERY_HEADS * HEAD_SIZE))
        scale = q_col[rows]
        for t in range(HEADS):
            unit = q_raw[rows, cols(t)].astype(F32) * scale
            qgrad[rows, cols(t)] = (scale * (u_all[rows, cols(t)] - unit * mean)).astype(BF16)
        qgrad_copy(b).start()

    def attend(b, biases, g):
        rows = block_rows(b)
        window = pl.ds(pl.multiple_of(b * BLOCK, BLOCK), WINDOW)
        gc = cols(g)
        queries = jnp.concatenate([qn[:, cols(g * GROUP + h)] for h in range(GROUP)], axis=0)
        grads = jnp.concatenate([go[rows, cols(g * GROUP + h)] for h in range(GROUP)], axis=0)
        scores = dot(kn[window, gc], queries, 1, 1)
        first = jnp.concatenate([tri[0]] * GROUP, axis=1)
        last = jnp.concatenate([tri[1]] * GROUP, axis=1)
        parts = [scores[c * BLOCK : (c + 1) * BLOCK] for c in range(WINDOW_BLOCKS)]
        parts[0] = parts[0] + first
        parts[-1] = parts[-1] + last
        top = None
        for part, bias in zip(parts, biases):
            here = jnp.max(part, axis=0, keepdims=True) + bias
            top = here if top is None else jnp.maximum(top, here)
        top = top * SCALE_LOG2
        expo = [
            jnp.exp2(part * SCALE_LOG2 - (top - bias)) for part, bias in zip(parts, biases)
        ]
        inverse = 1.0 / sum(jnp.sum(e, axis=0, keepdims=True) for e in expo)
        weights = jnp.concatenate([e * inverse for e in expo], axis=0)
        weights_low = weights.astype(BF16)
        dweights = dot(vals[window, gc], grads, 1, 1)
        delta = jnp.sum(weights * dweights, axis=0, keepdims=True)
        dscores_low = (weights * (dweights - delta)).astype(BF16)
        out_t = dot(v_t[gc, window], weights_low, 1, 0)
        dquery_t = dot(k_t[gc, window], dscores_low, 1, 0)
        dv[window, gc] += dot(weights_low, grads, 1, 0)
        dk[window, gc] += dot(dscores_low, queries, 1, 0)
        scale = q_col[rows]
        product = None
        for h in range(GROUP):
            hc = cols(g * GROUP + h)
            att[rows, hc] = out_t[:, cols(h)].T.astype(BF16)
            dquery = dquery_t[:, cols(h)].T * SCALE
            onto = dquery * (q_raw[rows, hc].astype(F32) * scale)
            q_acc[:, hc] += eight(onto)
            gain = q_gain[:, hc]
            u_all[rows, hc] = dquery * gain
            product = onto * gain if product is None else product + onto * gain
        return product

    def back_copies(b):
        rows = block_rows(b)
        return [
            remote(back_k.at[rows], got_k.at[rows], back_send.at[0, b], back_recv.at[0, b], ctx=prv),
            remote(back_v.at[rows], got_v.at[rows], back_send.at[1, b], back_recv.at[1, b], ctx=prv),
        ]

    def send_back(b):
        rows = block_rows(b)
        scale = k_col[rows]
        product = None
        for t in range(GROUPS):
            dkey = dk[rows, cols(t)] * SCALE
            onto = dkey * (k_raw[rows, cols(t)].astype(F32) * scale)
            k_acc[:, cols(t)] += eight(onto)
            back_k[rows, cols(t)] = dkey.astype(BF16)
            back_v[rows, cols(t)] = dv[rows, cols(t)].astype(BF16)
            gain = k_gain[:, cols(t)]
            product = onto * gain if product is None else product + onto * gain
        for copy in back_copies(b):
            copy.start()
        hin[pl.ds(b, 1), :] = row_sums(product)

    def exchange(src, dst, send, recv):
        return [
            remote(src, dst.at[head], send.at[r - 1], recv.at[r - 1], head=at_head(r))
            for r in range(1, 4)
        ]

    hin_copies = exchange(hin, hin_all, hin_send, hin_recv)

    def step(s, _):
        b = order(s)
        rows = block_rows(b)

        @pl.when(s == 3)
        def _():
            for copy in halo_copies:
                copy.wait_recv()
            relay.wait_recv()
            halo_scale = lax.rsqrt(halo_stat[...] / (KEY_VALUE_HEADS * HEAD_SIZE) + EPS)
            for n in range(HALO_BLOCKS):
                norm_keys(n, halo_scale[n + HALO_BLOCKS : n + HALO_BLOCKS + 1])
            lax.fori_loop(0, HALO_BLOCKS, turn_values, 0)

        here = ctx * BLOCKS_HERE + b
        doc = docs[here]
        biases = []
        for c in range(WINDOW_BLOCKS):
            there = here - HALO_BLOCKS + c
            same = (docs[jnp.maximum(there, 0)] == doc) & (there >= 0)
            biases.append(jnp.where(same, 0.0, NEGATIVE))

        scale = q_col[rows]
        for t in range(HEADS):
            unit = q_raw[rows, cols(t)].astype(F32) * scale
            qn[:, cols(t)] = (unit * q_gain[:, cols(t)]).astype(BF16)

        product = attend(b, biases, 0) + attend(b, biases, 1)
        att_copy(b).start()
        tile = jnp.broadcast_to(row_sums(product), (8, 128))
        inner[b] = tile
        inner_all[head, b] = tile
        for copy in inner_copies(b):
            copy.start()

        @pl.when((s >= 3) & (s < 7))
        def _():
            send_back(s - 3)

        @pl.when(s == 6)
        def _():
            hin_all[head] = hin[...]
            for copy in hin_copies:
                copy.start()

        @pl.when((s >= 1) & (s < 7))
        def _():
            finish_queries(order(s - 1))

        return 0

    hin[...] = jnp.zeros_like(hin)
    lax.fori_loop(0, BLOCKS_HERE, step, 0)

    def own_keys(b, _):
        rows = block_rows(b + HALO_BLOCKS)
        scale = k_col[rows]
        product = None
        for t in range(GROUPS):
            onto = dk[rows, cols(t)] * SCALE * (k_raw[rows, cols(t)].astype(F32) * scale)
            k_acc[:, cols(t)] += eight(onto)
            gain = k_gain[:, cols(t)]
            product = onto * gain if product is None else product + onto * gain
        kin[pl.ds(b, 1), :] = row_sums(product)
        return 0

    lax.fori_loop(0, BLOCKS_HERE, own_keys, 0)
    for t in range(HEADS):
        gains[t : t + 1] = jnp.sum(q_acc[:, cols(t)], axis=0, keepdims=True)
    for t in range(GROUPS):
        gains[HEADS + t : HEADS + t + 1] = jnp.sum(k_acc[:, cols(t)], axis=0, keepdims=True)
    gains[HEADS + GROUPS :] = jnp.zeros((GAIN_ROWS - HEADS - GROUPS, 128), F32)
    x_copies = [
        remote(gains, gains_x.at[x], gain_send.at[r - 1], gain_recv.at[r - 1], ctx=at_x(r))
        for r in range(1, 4)
    ]
    for copy in x_copies:
        copy.start()
    gains_x[x] = gains[...]
    kin_copies = exchange(kin, kin_all, kin_send, kin_recv)
    for copy in kin_copies:
        copy.start()
    kin_all[head] = kin[...]

    for copy in hin_copies:
        copy.wait_recv()
    hin_sum[...] = hin_all[0] + hin_all[1] + hin_all[2] + hin_all[3]
    hin_back = remote(hin_sum, hin_got, hin_send.at[3], hin_recv.at[3], ctx=prv)
    hin_back.start()

    finish_queries(3)

    for copy in x_copies:
        copy.wait_recv()
    mine = gains_x[0] + gains_x[1] + gains_x[2] + gains_x[3]
    gains_z[z] = mine
    z_copies = [
        remote(
            gains_z.at[z], gains_z.at[z], gain_send.at[r + 2], gain_recv.at[r + 2], ctx=at_z(r)
        )
        for r in range(1, 4)
    ]
    for copy in z_copies:
        copy.start()

    finish_queries(7)

    for copy in z_copies:
        copy.wait_recv()
    gains_y[y] = gains_z[0] + gains_z[1] + gains_z[2] + gains_z[3]
    y_copy = remote(gains_y.at[y], gains_y.at[y], gain_send.at[6], gain_recv.at[6], ctx=at_y)
    y_copy.start()

    for n in range(HALO_BLOCKS):
        for copy in back_copies(n):
            copy.wait_recv()
    split = TOKENS - HALO
    vgrad[0:split] = dv[HALO : HALO + split].astype(BF16)
    vgrad[split:] = (dv[HALO + split :] + got_v[...].astype(F32)).astype(BF16)
    v_copy = pltpu.make_async_copy(vgrad, vg_out, load_sem.at[4])
    v_copy.start()

    for copy in kin_copies:
        copy.wait_recv()
    hin_back.wait_recv()
    kin_total = kin_all[0] + kin_all[1] + kin_all[2] + kin_all[3]
    got_total = hin_got[...]
    for b in range(BLOCKS_HERE):
        there = slice(b * BLOCK, (b + 1) * BLOCK)
        rows = slice(HALO + b * BLOCK, HALO + (b + 1) * BLOCK)
        row = kin_total[b : b + 1]
        n = b - (BLOCKS_HERE - HALO_BLOCKS)
        if n >= 0:
            row = row + got_total[n : n + 1]
        mean = column(row / (KEY_VALUE_HEADS * HEAD_SIZE))
        scale = k_col[rows]
        for t in range(GROUPS):
            dkey = dk[rows, cols(t)] * SCALE
            if n >= 0:
                dkey = dkey + got_k[n * BLOCK : (n + 1) * BLOCK, cols(t)].astype(F32)
            unit = k_raw[rows, cols(t)].astype(F32) * scale
            grad = scale * (dkey * k_gain[:, cols(t)] - unit * mean)
            kgrad[there, cols(t)] = grad.astype(BF16)
    k_copy = pltpu.make_async_copy(kgrad, kg_out, load_sem.at[5])
    k_copy.start()

    y_copy.wait_recv()
    summed = gains_y[0] + gains_y[1]
    for t in range(HEADS):
        qgain_out[:, cols(t)] = summed[t : t + 1]
    for t in range(GROUPS):
        kgain_out[:, cols(t)] = summed[HEADS + t : HEADS + t + 1]

    for copy in (
        halo_copies + [relay] + stat_copies + hin_copies + [hin_back] + kin_copies
        + x_copies + z_copies + [y_copy]
    ):
        copy.wait_send()
    for n in range(HALO_BLOCKS):
        for copy in back_copies(n):
            copy.wait_send()

    def drain(b, _):
        for copy in inner_copies(b):
            copy.wait_send()
        att_copy(b).wait()
        qgrad_copy(b).wait()
        return 0

    lax.fori_loop(0, BLOCKS_HERE, drain, 0)
    v_copy.wait()
    k_copy.wait()


def local(query_raw, key_raw, values, output_gradient, query_gain, key_norm_gain, block_docs):
    hbm = pl.BlockSpec(memory_space=pl.ANY)
    vmem = pl.BlockSpec(memory_space=pltpu.VMEM)
    smem = pl.BlockSpec(memory_space=pltpu.SMEM)
    sems = pltpu.SemaphoreType.DMA
    stat = pltpu.VMEM((8, 128), F32)
    stats = pltpu.VMEM((HEAD_PEERS, 8, 128), F32)
    gain = pltpu.VMEM((GAIN_ROWS, 128), F32)
    scratch = [
        pltpu.VMEM((TOKENS, QCOLS), BF16),
        pltpu.VMEM((TOKENS, QCOLS), BF16),
        pltpu.VMEM((TOKENS, QCOLS), BF16),
        pltpu.VMEM((TOKENS, QCOLS), BF16),
        pltpu.VMEM((TOKENS, QCOLS), F32),
        pltpu.VMEM((BLOCK, QCOLS), BF16),
        pltpu.VMEM((EXT, KCOLS), BF16),
        pltpu.VMEM((EXT, KCOLS), BF16),
        pltpu.VMEM((EXT, KCOLS), BF16),
        pltpu.VMEM((KCOLS, EXT), BF16),
        pltpu.VMEM((KCOLS, EXT), BF16),
        pltpu.VMEM((EXT, KCOLS), F32),
        pltpu.VMEM((EXT, KCOLS), F32),
        pltpu.VMEM((HALO, KCOLS), BF16),
        pltpu.VMEM((HALO, KCOLS), BF16),
        pltpu.VMEM((HALO, KCOLS), BF16),
        pltpu.VMEM((HALO, KCOLS), BF16),
        pltpu.VMEM((TOKENS, KCOLS), BF16),
        pltpu.VMEM((TOKENS, KCOLS), BF16),
        pltpu.VMEM((TOKENS, 128), F32),
        pltpu.VMEM((EXT, 128), F32),
        pltpu.VMEM((2, BLOCK, BLOCK), F32),
        pltpu.VMEM((16, 128), F32),
        pltpu.VMEM((HEAD_PEERS, 16, 128), F32),
        stat,
        stat,
        pltpu.VMEM((BLOCKS_HERE, 8, 128), F32),
        pltpu.VMEM((HEAD_PEERS, BLOCKS_HERE, 8, 128), F32),
        stat,
        stats,
        stat,
        stats,
        stat,
        stat,
        pltpu.VMEM((8, QCOLS), F32),
        pltpu.VMEM((8, KCOLS), F32),
        gain,
        pltpu.VMEM((4, GAIN_ROWS, 128), F32),
        pltpu.VMEM((4, GAIN_ROWS, 128), F32),
        pltpu.VMEM((2, GAIN_ROWS, 128), F32),
        sems((6,)),
        sems((2, BLOCKS_HERE)),
        sems((3,)),
        sems((3,)),
        sems((3,)),
        sems((3,)),
        sems((3, BLOCKS_HERE)),
        sems((3, BLOCKS_HERE)),
        sems((2, HALO_BLOCKS)),
        sems((2, HALO_BLOCKS)),
        sems((3,)),
        sems((3,)),
        sems((4,)),
        sems((4,)),
        sems((7,)),
        sems((7,)),
    ]
    shape = jax.ShapeDtypeStruct
    outs = pl.pallas_call(
        kernel,
        out_shape=[
            shape((TOKENS, QCOLS), BF16),
            shape((TOKENS, QCOLS), BF16),
            shape((TOKENS, KCOLS), BF16),
            shape((TOKENS, KCOLS), BF16),
            shape((1, QCOLS), F32),
            shape((1, KCOLS), F32),
        ],
        in_specs=[hbm] * 4 + [vmem] * 2 + [smem],
        out_specs=[hbm] * 4 + [vmem] * 2,
        scratch_shapes=scratch,
        compiler_params=pltpu.CompilerParams(
            collective_id=0, has_side_effects=True, vmem_limit_bytes=58 * 2**20
        ),
        cost_estimate=pl.CostEstimate(
            flops=8_000_000_000, bytes_accessed=10_000_000, transcendentals=5_000_000
        ),
    )(
        query_raw, key_raw, values, output_gradient,
        query_gain.reshape(1, QCOLS), key_norm_gain.reshape(1, KCOLS), block_docs,
    )
    return (*outs[:4], outs[4].reshape(QCOLS), outs[5].reshape(KCOLS))


def solution(mesh):
    placed = (
        P("ctx", "head"),
        P("ctx", "head"),
        P("ctx", "head"),
        P("ctx", "head"),
        P("head"),
        P("head"),
        P(),
    )
    return jax.shard_map(
        local,
        mesh=mesh,
        in_specs=placed,
        out_specs=(
            P("ctx", "head"),
            P("ctx", "head"),
            P("ctx", "head"),
            P("ctx", "head"),
            P("head"),
            P("head"),
        ),
        check_vma=False,
    )
```

```python
import jax
import jax.numpy as jnp
from jax import lax
from jax.experimental import pallas as pl
from jax.experimental.pallas import tpu as pltpu
from jax.sharding import PartitionSpec as P

QUERY_HEADS = 32
KEY_VALUE_HEADS = 8
HEAD_SIZE = 128
WINDOW_REACH = 512
BLOCK = 128
EPS = 1e-06
NEGATIVE = -1e30
SCALE = HEAD_SIZE ** (-0.5)
SCALE_LOG2 = SCALE * 1.4426950408889634

F32 = jnp.float32
BF16 = jnp.bfloat16
MESH = pl.DeviceIdType.MESH

TOKENS = 1024
BLOCKS_HERE = TOKENS // BLOCK
HALO = WINDOW_REACH
HALO_BLOCKS = HALO // BLOCK
WINDOW_BLOCKS = HALO_BLOCKS + 1
WINDOW = WINDOW_BLOCKS * BLOCK
EXT = HALO + TOKENS
GROUPS = 2
GROUP = 4
PAIR = 2
HEADS = GROUPS * GROUP
QCOLS = HEADS * HEAD_SIZE
KCOLS = GROUPS * HEAD_SIZE
HEAD_PEERS = 4
GAIN_ROWS = 16


def dot(a, b, ca, cb):
    return lax.dot_general(a, b, (((ca,), (cb,)), ((), ())), preferred_element_type=F32)


def block_rows(b):
    return pl.ds(pl.multiple_of(b * BLOCK, BLOCK), BLOCK)


def cols(t):
    return slice(t * 128, (t + 1) * 128)


def column(row):
    return jnp.broadcast_to(row, (128, 128)).T


def row_sums(tile):
    return jnp.sum(tile.T, axis=0, keepdims=True)


def eight(tile):
    return jnp.sum(tile.reshape(16, 8, tile.shape[1]), axis=0)


def kernel(
    q_in, k_in, v_in, g_in, q_gain, k_gain, docs,
    att, qgrad, kgrad, vgrad, qgain_out, kgain_out,
    q_raw, go, u_all, qn,
    k_raw, vals, kn, k_t, v_t, dk, dv,
    back_k, back_v, got_k, got_v,
    q_col, k_col, tri,
    stat, stat_all, k_stat, halo_stat,
    inner, inner_all, kin, kin_all, hin, hin_all, hin_sum, hin_got,
    q_acc, k_acc, products, gains, gains_x, gains_zy,
    load_sem, halo_send, halo_recv, stat_send, stat_recv,
    inner_send, inner_recv, back_send, back_recv, kin_send, kin_recv,
    hin_send, hin_recv, gain_send, gain_recv,
):
    ctx = lax.axis_index("ctx")
    head = lax.axis_index("head")
    x = ctx % 4
    z = (ctx // 4) % 4
    y = ctx // 16
    nxt = (ctx + 1) % 32
    prv = (ctx + 31) % 32

    def at_x(r):
        return (y * 4 + z) * 4 + (x + r) % 4

    zy = y * 4 + z

    def at_zy(r):
        return ((zy + r) % 8) * 4 + x

    def at_head(r):
        return (head + r) % HEAD_PEERS

    def remote(src, dst, send, recv, **where):
        return pltpu.make_async_remote_copy(
            src_ref=src, dst_ref=dst, send_sem=send, recv_sem=recv,
            device_id=where, device_id_type=MESH,
        )

    barrier = pltpu.get_barrier_semaphore()
    for r in range(1, 4):
        pl.semaphore_signal(barrier, inc=1, device_id={"head": at_head(r)}, device_id_type=MESH)
        pl.semaphore_signal(barrier, inc=1, device_id={"ctx": at_x(r)}, device_id_type=MESH)
    for r in range(1, 8):
        pl.semaphore_signal(barrier, inc=1, device_id={"ctx": at_zy(r)}, device_id_type=MESH)
    for other in (nxt, prv):
        pl.semaphore_signal(barrier, inc=1, device_id={"ctx": other}, device_id_type=MESH)

    own = pl.ds(HALO, TOKENS)
    load_k = pltpu.make_async_copy(k_in, k_raw.at[own], load_sem.at[0])
    load_q = pltpu.make_async_copy(q_in, q_raw, load_sem.at[1])
    load_v = pltpu.make_async_copy(v_in, vals.at[own], load_sem.at[2])
    load_g = pltpu.make_async_copy(g_in, go, load_sem.at[3])
    load_k.start()
    load_q.start()
    load_v.start()
    load_g.start()

    load_k.wait()
    load_q.wait()

    for b in range(BLOCKS_HERE):
        rows = slice(b * BLOCK, (b + 1) * BLOCK)
        total = None
        for t in range(HEADS):
            part = q_raw[rows, cols(t)].astype(F32)
            total = part * part if total is None else total + part * part
        stat[b : b + 1] = row_sums(total)
        rows = slice(HALO + b * BLOCK, HALO + (b + 1) * BLOCK)
        total = None
        for t in range(GROUPS):
            part = k_raw[rows, cols(t)].astype(F32)
            total = part * part if total is None else total + part * part
        stat[b + 8 : b + 9] = row_sums(total)

    pl.semaphore_wait(barrier, 15)
    stat_copies = [
        remote(stat, stat_all.at[head], stat_send.at[r - 1], stat_recv.at[r - 1], head=at_head(r))
        for r in range(1, 4)
    ]
    for copy in stat_copies:
        copy.start()
    stat_all[head] = stat[...]

    def halo_copies(n):
        there = pl.ds(TOKENS - HALO + n * BLOCK, BLOCK)
        here = pl.ds(n * BLOCK, BLOCK)
        return [
            remote(k_in.at[there], k_raw.at[here], halo_send.at[n], halo_recv.at[n], ctx=nxt),
            remote(
                v_in.at[there], vals.at[here], halo_send.at[4 + n], halo_recv.at[4 + n], ctx=nxt
            ),
        ]

    for n in reversed(range(HALO_BLOCKS)):
        for copy in halo_copies(n):
            copy.start()

    key_at = lax.broadcasted_iota(jnp.int32, (BLOCK, BLOCK), 0)
    query_at = lax.broadcasted_iota(jnp.int32, (BLOCK, BLOCK), 1)
    tri[0] = jnp.where(key_at > query_at, 0.0, NEGATIVE)
    tri[1] = jnp.where(key_at <= query_at, 0.0, NEGATIVE)
    dk[...] = jnp.zeros_like(dk)
    dv[...] = jnp.zeros_like(dv)
    q_acc[...] = jnp.zeros_like(q_acc)
    k_acc[...] = jnp.zeros_like(k_acc)
    load_v.wait()

    def turn_values(b, _):
        rows = block_rows(b)
        for t in range(GROUPS):
            v_t[cols(t), rows] = vals[rows, cols(t)].T
        return 0

    lax.fori_loop(HALO_BLOCKS, EXT // BLOCK, turn_values, 0)

    for copy in stat_copies:
        copy.wait_recv()
    total = stat_all[0] + stat_all[1] + stat_all[2] + stat_all[3]
    k_stat[...] = total[8:16]
    relay = remote(k_stat, halo_stat, halo_send.at[8], halo_recv.at[8], ctx=nxt)
    relay.start()

    q_scale = lax.rsqrt(total[0:8] / (QUERY_HEADS * HEAD_SIZE) + EPS)
    for b in range(BLOCKS_HERE):
        q_col[b * BLOCK : (b + 1) * BLOCK] = column(q_scale[b : b + 1])

    def norm_keys(b, scale_row):
        rows = slice(b * BLOCK, (b + 1) * BLOCK)
        scale = column(scale_row)
        k_col[rows] = scale
        for t in range(GROUPS):
            unit = k_raw[rows, cols(t)].astype(F32) * scale
            normed = (unit * k_gain[:, cols(t)]).astype(BF16)
            kn[rows, cols(t)] = normed
            k_t[cols(t), rows] = normed.T

    k_scale = lax.rsqrt(total[8:16] / (KEY_VALUE_HEADS * HEAD_SIZE) + EPS)
    for b in range(BLOCKS_HERE):
        norm_keys(b + HALO_BLOCKS, k_scale[b : b + 1])
    load_g.wait()

    def order(s):
        return jnp.where(s < 3, s + 4, jnp.where(s == 3, 3, jnp.where(s < 7, s - 4, 7)))

    def inner_copies(b):
        return [
            remote(
                inner.at[b], inner_all.at[head, b],
                inner_send.at[r - 1, b], inner_recv.at[r - 1, b], head=at_head(r),
            )
            for r in range(1, 4)
        ]

    def finish_queries(b):
        rows = block_rows(b)
        for copy in inner_copies(b):
            copy.wait_recv()
        summed = inner_all[0, b] + inner_all[1, b] + inner_all[2, b] + inner_all[3, b]
        mean = column(summed[0:1] / (QUERY_HEADS * HEAD_SIZE))
        scale = q_col[rows]
        for t in range(HEADS):
            unit = q_raw[rows, cols(t)].astype(F32) * scale
            qgrad[rows, cols(t)] = (scale * (u_all[rows, cols(t)] - unit * mean)).astype(BF16)

    def attend(b, biases):
        rows = block_rows(b)
        window = pl.ds(pl.multiple_of(b * BLOCK, BLOCK), WINDOW)
        first = jnp.concatenate([tri[0]] * PAIR, axis=1)
        last = jnp.concatenate([tri[1]] * PAIR, axis=1)
        scale = q_col[rows]

        def products_in(g, h):
            queries = jnp.concatenate([qn[:, cols(h + n)] for n in range(PAIR)], axis=0)
            grads = jnp.concatenate([go[rows, cols(h + n)] for n in range(PAIR)], axis=0)
            scores = dot(kn[window, cols(g)], queries, 1, 1)
            dweights = dot(vals[window, cols(g)], grads, 1, 1)
            return queries, grads, scores, dweights

        def softmax(scores, dweights):
            parts = [scores[c * BLOCK : (c + 1) * BLOCK] for c in range(WINDOW_BLOCKS)]
            parts[0] = parts[0] + first
            parts[-1] = parts[-1] + last
            top = None
            for part, bias in zip(parts, biases):
                here = jnp.max(part, axis=0, keepdims=True) + bias
                top = here if top is None else jnp.maximum(top, here)
            top = top * SCALE_LOG2
            expo = [
                jnp.exp2(part * SCALE_LOG2 - (top - bias)) for part, bias in zip(parts, biases)
            ]
            inverse = 1.0 / sum(jnp.sum(e, axis=0, keepdims=True) for e in expo)
            weights = jnp.concatenate([e * inverse for e in expo], axis=0)
            delta = jnp.sum(weights * dweights, axis=0, keepdims=True)
            return weights.astype(BF16), (weights * (dweights - delta)).astype(BF16)

        def products_out(g, h, queries, grads, weights_low, dscores_low):
            gc = cols(g)
            out_t = dot(v_t[gc, window], weights_low, 1, 0)
            dquery_t = dot(k_t[gc, window], dscores_low, 1, 0)
            dv[window, gc] += dot(weights_low, grads, 1, 0)
            dk[window, gc] += dot(dscores_low, queries, 1, 0)
            product = None
            for n in range(PAIR):
                hc = cols(h + n)
                att[rows, hc] = out_t[:, cols(n)].T.astype(BF16)
                dquery = dquery_t[:, cols(n)].T * SCALE
                onto = dquery * (q_raw[rows, hc].astype(F32) * scale)
                q_acc[:, hc] += eight(onto)
                gain = q_gain[:, hc]
                u_all[rows, hc] = dquery * gain
                product = onto * gain if product is None else product + onto * gain
            return product

        units = [(h // GROUP, h) for h in range(0, HEADS, PAIR)]
        product = None
        ahead = products_in(*units[0])
        for n, unit in enumerate(units):
            queries, grads, scores, dweights = ahead
            if n + 1 < len(units):
                ahead = products_in(*units[n + 1])
            low = softmax(scores, dweights)
            part = products_out(*unit, queries, grads, *low)
            product = part if product is None else product + part
        return product

    def back_copies(b):
        rows = block_rows(b)
        return [
            remote(back_k.at[rows], got_k.at[rows], back_send.at[0, b], back_recv.at[0, b], ctx=prv),
            remote(back_v.at[rows], got_v.at[rows], back_send.at[1, b], back_recv.at[1, b], ctx=prv),
        ]

    def send_back(b):
        rows = block_rows(b)
        scale = k_col[rows]
        product = None
        for t in range(GROUPS):
            dkey = dk[rows, cols(t)] * SCALE
            onto = dkey * (k_raw[rows, cols(t)].astype(F32) * scale)
            k_acc[:, cols(t)] += eight(onto)
            back_k[rows, cols(t)] = dkey.astype(BF16)
            back_v[rows, cols(t)] = dv[rows, cols(t)].astype(BF16)
            gain = k_gain[:, cols(t)]
            product = onto * gain if product is None else product + onto * gain
        for copy in back_copies(b):
            copy.start()
        hin[pl.ds(b, 1), :] = row_sums(product)

    def exchange(src, dst, send, recv):
        return [
            remote(src, dst.at[head], send.at[r - 1], recv.at[r - 1], head=at_head(r))
            for r in range(1, 4)
        ]

    hin_copies = exchange(hin, hin_all, hin_send, hin_recv)

    def step(s, _):
        b = order(s)
        rows = block_rows(b)

        def take_halo(n):
            for copy in halo_copies(n):
                copy.wait_recv()
            halo_scale = lax.rsqrt(halo_stat[...] / (KEY_VALUE_HEADS * HEAD_SIZE) + EPS)
            norm_keys(n, halo_scale[n + HALO_BLOCKS : n + HALO_BLOCKS + 1])
            turn_values(n, 0)

        @pl.when(s == 3)
        def _():
            relay.wait_recv()
            take_halo(3)

        @pl.when(s == 4)
        def _():
            for n in range(3):
                take_halo(n)

        here = ctx * BLOCKS_HERE + b
        doc = docs[here]
        biases = []
        for c in range(WINDOW_BLOCKS):
            there = here - HALO_BLOCKS + c
            same = (docs[jnp.maximum(there, 0)] == doc) & (there >= 0)
            biases.append(jnp.where(same, 0.0, NEGATIVE))

        scale = q_col[rows]
        for t in range(HEADS):
            unit = q_raw[rows, cols(t)].astype(F32) * scale
            qn[:, cols(t)] = (unit * q_gain[:, cols(t)]).astype(BF16)

        product = attend(b, biases)
        tile = jnp.broadcast_to(row_sums(product), (8, 128))
        inner[b] = tile
        inner_all[head, b] = tile
        for copy in inner_copies(b):
            copy.start()

        @pl.when((s >= 4) & (s < 7))
        def _():
            send_back(s - 4)

        @pl.when(s == 6)
        def _():
            send_back(3)
            hin_all[head] = hin[...]
            for copy in hin_copies:
                copy.start()

        @pl.when(s >= 4)
        def _():
            finish_queries(order(s - 4))

        return 0

    hin[...] = jnp.zeros_like(hin)
    lax.fori_loop(0, BLOCKS_HERE, step, 0)

    for b in range(BLOCKS_HERE):
        rows = slice(HALO + b * BLOCK, HALO + (b + 1) * BLOCK)
        scale = k_col[rows]
        product = None
        for t in range(GROUPS):
            onto = dk[rows, cols(t)] * SCALE * (k_raw[rows, cols(t)].astype(F32) * scale)
            k_acc[:, cols(t)] += eight(onto)
            gain = k_gain[:, cols(t)]
            product = onto * gain if product is None else product + onto * gain
        products[b] = product

    for t in range(HEADS):
        gains[t : t + 1] = jnp.sum(q_acc[:, cols(t)], axis=0, keepdims=True)
    for t in range(GROUPS):
        gains[HEADS + t : HEADS + t + 1] = jnp.sum(k_acc[:, cols(t)], axis=0, keepdims=True)
    gains[HEADS + GROUPS :] = jnp.zeros((GAIN_ROWS - HEADS - GROUPS, 128), F32)
    x_copies = [
        remote(gains, gains_x.at[x], gain_send.at[r - 1], gain_recv.at[r - 1], ctx=at_x(r))
        for r in range(1, 4)
    ]
    for copy in x_copies:
        copy.start()
    gains_x[x] = gains[...]
    for b in range(BLOCKS_HERE):
        kin[b : b + 1] = row_sums(products[b])
    kin_copies = exchange(kin, kin_all, kin_send, kin_recv)
    for copy in kin_copies:
        copy.start()
    kin_all[head] = kin[...]

    for copy in hin_copies:
        copy.wait_recv()
    hin_sum[...] = hin_all[0] + hin_all[1] + hin_all[2] + hin_all[3]
    hin_back = remote(hin_sum, hin_got, hin_send.at[3], hin_recv.at[3], ctx=prv)
    hin_back.start()

    for copy in x_copies:
        copy.wait_recv()
    gains_zy[zy] = gains_x[0] + gains_x[1] + gains_x[2] + gains_x[3]
    zy_copies = [
        remote(
            gains_zy.at[zy], gains_zy.at[zy], gain_send.at[r + 2], gain_recv.at[r + 2], ctx=at_zy(r)
        )
        for r in range(1, 8)
    ]
    for copy in zy_copies:
        copy.start()

    def finish_later(s, _):
        finish_queries(order(s))
        return 0

    lax.fori_loop(4, BLOCKS_HERE, finish_later, 0)

    for n in range(HALO_BLOCKS):
        for copy in back_copies(n):
            copy.wait_recv()
    split = TOKENS - HALO
    vgrad[0:split] = dv[HALO : HALO + split].astype(BF16)
    vgrad[split:] = (dv[HALO + split :] + got_v[...].astype(F32)).astype(BF16)

    for copy in kin_copies:
        copy.wait_recv()
    hin_back.wait_recv()
    kin_total = kin_all[0] + kin_all[1] + kin_all[2] + kin_all[3]
    got_total = hin_got[...]
    for b in range(BLOCKS_HERE):
        there = slice(b * BLOCK, (b + 1) * BLOCK)
        rows = slice(HALO + b * BLOCK, HALO + (b + 1) * BLOCK)
        row = kin_total[b : b + 1]
        n = b - (BLOCKS_HERE - HALO_BLOCKS)
        if n >= 0:
            row = row + got_total[n : n + 1]
        mean = column(row / (KEY_VALUE_HEADS * HEAD_SIZE))
        scale = k_col[rows]
        for t in range(GROUPS):
            dkey = dk[rows, cols(t)] * SCALE
            if n >= 0:
                dkey = dkey + got_k[n * BLOCK : (n + 1) * BLOCK, cols(t)].astype(F32)
            unit = k_raw[rows, cols(t)].astype(F32) * scale
            grad = scale * (dkey * k_gain[:, cols(t)] - unit * mean)
            kgrad[there, cols(t)] = grad.astype(BF16)

    for copy in zy_copies:
        copy.wait_recv()
    summed = gains_zy[0]
    for n in range(1, 8):
        summed = summed + gains_zy[n]
    for t in range(HEADS):
        qgain_out[:, cols(t)] = summed[t : t + 1]
    for t in range(GROUPS):
        kgain_out[:, cols(t)] = summed[HEADS + t : HEADS + t + 1]

    for copy in (
        [relay] + stat_copies + hin_copies + [hin_back] + kin_copies + x_copies + zy_copies
    ):
        copy.wait_send()
    for n in range(HALO_BLOCKS):
        for copy in halo_copies(n) + back_copies(n):
            copy.wait_send()

    def drain(b, _):
        for copy in inner_copies(b):
            copy.wait_send()
        return 0

    lax.fori_loop(0, BLOCKS_HERE, drain, 0)


def write(*refs):
    *pairs, sem = refs
    half = len(pairs) // 2
    copies = [
        pltpu.make_async_copy(src, dst, sem.at[n])
        for n, (src, dst) in enumerate(zip(pairs[:half], pairs[half:]))
    ]
    for copy in copies:
        copy.start()
    for copy in copies:
        copy.wait()


def local(query_raw, key_raw, values, output_gradient, query_gain, key_norm_gain, block_docs):
    hbm = pl.BlockSpec(memory_space=pltpu.HBM)
    vmem = pl.BlockSpec(memory_space=pltpu.VMEM)
    smem = pl.BlockSpec(memory_space=pltpu.SMEM)
    sems = pltpu.SemaphoreType.DMA
    stat = pltpu.VMEM((8, 128), F32)
    stats = pltpu.VMEM((HEAD_PEERS, 8, 128), F32)
    gain = pltpu.VMEM((GAIN_ROWS, 128), F32)
    scratch = [
        pltpu.VMEM((TOKENS, QCOLS), BF16),
        pltpu.VMEM((TOKENS, QCOLS), BF16),
        pltpu.VMEM((TOKENS, QCOLS), F32),
        pltpu.VMEM((BLOCK, QCOLS), BF16),
        pltpu.VMEM((EXT, KCOLS), BF16),
        pltpu.VMEM((EXT, KCOLS), BF16),
        pltpu.VMEM((EXT, KCOLS), BF16),
        pltpu.VMEM((KCOLS, EXT), BF16),
        pltpu.VMEM((KCOLS, EXT), BF16),
        pltpu.VMEM((EXT, KCOLS), F32),
        pltpu.VMEM((EXT, KCOLS), F32),
        pltpu.VMEM((HALO, KCOLS), BF16),
        pltpu.VMEM((HALO, KCOLS), BF16),
        pltpu.VMEM((HALO, KCOLS), BF16),
        pltpu.VMEM((HALO, KCOLS), BF16),
        pltpu.VMEM((TOKENS, 128), F32),
        pltpu.VMEM((EXT, 128), F32),
        pltpu.VMEM((2, BLOCK, BLOCK), F32),
        pltpu.VMEM((16, 128), F32),
        pltpu.VMEM((HEAD_PEERS, 16, 128), F32),
        stat,
        stat,
        pltpu.VMEM((BLOCKS_HERE, 8, 128), F32),
        pltpu.VMEM((HEAD_PEERS, BLOCKS_HERE, 8, 128), F32),
        stat,
        stats,
        stat,
        stats,
        stat,
        stat,
        pltpu.VMEM((8, QCOLS), F32),
        pltpu.VMEM((8, KCOLS), F32),
        pltpu.VMEM((BLOCKS_HERE, 128, 128), F32),
        gain,
        pltpu.VMEM((4, GAIN_ROWS, 128), F32),
        pltpu.VMEM((8, GAIN_ROWS, 128), F32),
        sems((4,)),
        sems((9,)),
        sems((9,)),
        sems((3,)),
        sems((3,)),
        sems((3, BLOCKS_HERE)),
        sems((3, BLOCKS_HERE)),
        sems((2, HALO_BLOCKS)),
        sems((2, HALO_BLOCKS)),
        sems((3,)),
        sems((3,)),
        sems((4,)),
        sems((4,)),
        sems((10,)),
        sems((10,)),
    ]
    shapes = [
        ((TOKENS, QCOLS), BF16),
        ((TOKENS, QCOLS), BF16),
        ((TOKENS, KCOLS), BF16),
        ((TOKENS, KCOLS), BF16),
        ((1, QCOLS), F32),
        ((1, KCOLS), F32),
    ]
    held = pl.pallas_call(
        kernel,
        out_shape=[pltpu.VMEM(*shape) for shape in shapes],
        in_specs=[hbm] * 4 + [vmem] * 2 + [smem],
        out_specs=[vmem] * 6,
        scratch_shapes=scratch,
        compiler_params=pltpu.CompilerParams(
            collective_id=0, has_side_effects=True, vmem_limit_bytes=56 * 2**20
        ),
        cost_estimate=pl.CostEstimate(
            flops=8_000_000_000, bytes_accessed=10_000_000, transcendentals=5_000_000
        ),
    )(
        query_raw, key_raw, values, output_gradient,
        query_gain.reshape(1, QCOLS), key_norm_gain.reshape(1, KCOLS), block_docs,
    )
    outs = pl.pallas_call(
        write,
        out_shape=[jax.ShapeDtypeStruct(*shape) for shape in shapes],
        in_specs=[vmem] * 6,
        out_specs=[hbm] * 6,
        scratch_shapes=[sems((6,))],
        compiler_params=pltpu.CompilerParams(vmem_limit_bytes=16 * 2**20),
    )(*[pltpu.with_memory_space_constraint(x, pltpu.VMEM) for x in held])
    return (*outs[:4], outs[4].reshape(QCOLS), outs[5].reshape(KCOLS))


def solution(mesh):
    placed = (
        P("ctx", "head"),
        P("ctx", "head"),
        P("ctx", "head"),
        P("ctx", "head"),
        P("head"),
        P("head"),
        P(),
    )
    return jax.shard_map(
        local,
        mesh=mesh,
        in_specs=placed,
        out_specs=(
            P("ctx", "head"),
            P("ctx", "head"),
            P("ctx", "head"),
            P("ctx", "head"),
            P("head"),
            P("head"),
        ),
        check_vma=False,
    )
```

```python
import jax
import jax.numpy as jnp
from jax import lax
from jax.experimental import pallas as pl
from jax.experimental.pallas import tpu as pltpu
from jax.sharding import PartitionSpec as P

QUERY_HEADS = 32
KEY_VALUE_HEADS = 8
HEAD_SIZE = 128
WINDOW_REACH = 512
BLOCK = 128
EPS = 1e-06
NEGATIVE = -1e30
SCALE = HEAD_SIZE ** (-0.5)
SCALE_LOG2 = SCALE * 1.4426950408889634

F32 = jnp.float32
BF16 = jnp.bfloat16
MESH = pl.DeviceIdType.MESH

TOKENS = 1024
BLOCKS_HERE = TOKENS // BLOCK
HALO = WINDOW_REACH
HALO_BLOCKS = HALO // BLOCK
WINDOW_BLOCKS = HALO_BLOCKS + 1
WINDOW = WINDOW_BLOCKS * BLOCK
EXT = HALO + TOKENS
GROUPS = 2
GROUP = 4
PAIR = 2
QUERY_PIECES = 4
HEADS = GROUPS * GROUP
QCOLS = HEADS * HEAD_SIZE
KCOLS = GROUPS * HEAD_SIZE
HEAD_PEERS = 4
GAIN_ROWS = 16


def dot(a, b, ca, cb):
    return lax.dot_general(a, b, (((ca,), (cb,)), ((), ())), preferred_element_type=F32)


def block_rows(b):
    return pl.ds(pl.multiple_of(b * BLOCK, BLOCK), BLOCK)


def cols(t):
    return slice(t * 128, (t + 1) * 128)


def column(row):
    return jnp.broadcast_to(row, (128, 128)).T


def row_sums(tile):
    return jnp.sum(tile.T, axis=0, keepdims=True)


def eight(tile):
    return jnp.sum(tile.reshape(16, 8, tile.shape[1]), axis=0)


def kernel(
    q_in, k_in, v_in, g_in, q_gain, k_gain, docs,
    att, qgrad, kgrad, vgrad, qgain_out, kgain_out,
    q_raw, go, u_all, qn,
    k_raw, vals, kn, k_t, v_t, dk, dv,
    back_k, back_v, got_k, got_v,
    q_col, k_col, tri, near, far,
    stat, stat_all, k_stat, halo_stat,
    inner, inner_all, kin, kin_all, hin, hin_all, hin_sum, hin_got,
    q_acc, k_acc, products, gains, gains_x, gains_zy,
    load_sem, halo_send, halo_recv, stat_send, stat_recv,
    inner_send, inner_recv, back_send, back_recv, kin_send, kin_recv,
    hin_send, hin_recv, gain_send, gain_recv,
):
    ctx = lax.axis_index("ctx")
    head = lax.axis_index("head")
    x = ctx % 4
    z = (ctx // 4) % 4
    y = ctx // 16
    nxt = (ctx + 1) % 32
    prv = (ctx + 31) % 32

    def at_x(r):
        return (y * 4 + z) * 4 + (x + r) % 4

    zy = y * 4 + z

    def at_zy(r):
        return ((zy + r) % 8) * 4 + x

    def at_head(r):
        return (head + r) % HEAD_PEERS

    def remote(src, dst, send, recv, **where):
        return pltpu.make_async_remote_copy(
            src_ref=src, dst_ref=dst, send_sem=send, recv_sem=recv,
            device_id=where, device_id_type=MESH,
        )

    own = pl.ds(HALO, TOKENS)
    load_k = pltpu.make_async_copy(k_in, k_raw.at[own], load_sem.at[0])
    load_v = pltpu.make_async_copy(v_in, vals.at[own], load_sem.at[1])
    load_g = pltpu.make_async_copy(g_in, go, load_sem.at[2])
    load_q = []
    for n in range(QUERY_PIECES):
        rows = pl.ds(n * (TOKENS // QUERY_PIECES), TOKENS // QUERY_PIECES)
        load_q.append(pltpu.make_async_copy(q_in.at[rows], q_raw.at[rows], load_sem.at[3 + n]))
    for copy in load_q:
        copy.start()
    load_k.start()

    barrier = pltpu.get_barrier_semaphore()
    for r in range(1, 4):
        pl.semaphore_signal(barrier, inc=1, device_id={"head": at_head(r)}, device_id_type=MESH)
        pl.semaphore_signal(barrier, inc=1, device_id={"ctx": at_x(r)}, device_id_type=MESH)
    for r in range(1, 8):
        pl.semaphore_signal(barrier, inc=1, device_id={"ctx": at_zy(r)}, device_id_type=MESH)
    for other in (nxt, prv):
        pl.semaphore_signal(barrier, inc=1, device_id={"ctx": other}, device_id_type=MESH)

    def halo_copies(n):
        there = pl.ds(TOKENS - HALO + n * BLOCK, BLOCK)
        here = pl.ds(n * BLOCK, BLOCK)
        return [
            remote(k_in.at[there], k_raw.at[here], halo_send.at[n], halo_recv.at[n], ctx=nxt),
            remote(
                v_in.at[there], vals.at[here], halo_send.at[4 + n], halo_recv.at[4 + n], ctx=nxt
            ),
        ]

    def send_halo(*chunks):
        for n in chunks:
            for copy in halo_copies(n):
                copy.start()

    for b in range(BLOCKS_HERE):
        if b % (BLOCKS_HERE // QUERY_PIECES) == 0:
            load_q[b * QUERY_PIECES // BLOCKS_HERE].wait()
        rows = slice(b * BLOCK, (b + 1) * BLOCK)
        total = None
        for t in range(HEADS):
            part = q_raw[rows, cols(t)].astype(F32)
            total = part * part if total is None else total + part * part
        stat[b : b + 1] = row_sums(total)
    load_k.wait()
    load_v.start()
    load_g.start()
    for b in range(BLOCKS_HERE):
        rows = slice(HALO + b * BLOCK, HALO + (b + 1) * BLOCK)
        total = None
        for t in range(GROUPS):
            part = k_raw[rows, cols(t)].astype(F32)
            total = part * part if total is None else total + part * part
        stat[b + 8 : b + 9] = row_sums(total)

    pl.semaphore_wait(barrier, 15)
    stat_copies = [
        remote(stat, stat_all.at[head], stat_send.at[r - 1], stat_recv.at[r - 1], head=at_head(r))
        for r in range(1, 4)
    ]
    for copy in stat_copies:
        copy.start()
    stat_all[head] = stat[...]

    send_halo(3)

    key_at = lax.broadcasted_iota(jnp.int32, (BLOCK, BLOCK), 0)
    query_at = lax.broadcasted_iota(jnp.int32, (BLOCK, BLOCK), 1)
    lower = jnp.where(key_at <= query_at, 1.0, 0.0)
    tri[...] = jnp.concatenate([lower] * PAIR, axis=1)
    near[...] = jnp.concatenate([lower] * PAIR, axis=1).astype(BF16)
    far[...] = (1.0 - jnp.concatenate([lower] * PAIR, axis=1)).astype(BF16)
    dk[...] = jnp.zeros_like(dk)
    dv[...] = jnp.zeros_like(dv)
    q_acc[...] = jnp.zeros_like(q_acc)
    k_acc[...] = jnp.zeros_like(k_acc)
    load_v.wait()

    def turn_values(b, _):
        rows = block_rows(b)
        for t in range(GROUPS):
            v_t[cols(t), rows] = vals[rows, cols(t)].T
        return 0

    lax.fori_loop(HALO_BLOCKS, EXT // BLOCK, turn_values, 0)

    for copy in stat_copies:
        copy.wait_recv()
    total = stat_all[0] + stat_all[1] + stat_all[2] + stat_all[3]
    k_stat[...] = total[8:16]
    relay = remote(k_stat, halo_stat, halo_send.at[8], halo_recv.at[8], ctx=nxt)
    relay.start()
    send_halo(2, 1, 0)

    q_scale = lax.rsqrt(total[0:8] / (QUERY_HEADS * HEAD_SIZE) + EPS)
    for b in range(BLOCKS_HERE):
        q_col[b * BLOCK : (b + 1) * BLOCK] = column(q_scale[b : b + 1])

    def norm_keys(b, scale_row):
        rows = slice(b * BLOCK, (b + 1) * BLOCK)
        scale = column(scale_row)
        k_col[rows] = scale
        for t in range(GROUPS):
            unit = k_raw[rows, cols(t)].astype(F32) * scale
            normed = (unit * k_gain[:, cols(t)]).astype(BF16)
            kn[rows, cols(t)] = normed
            k_t[cols(t), rows] = normed.T

    k_scale = lax.rsqrt(total[8:16] / (KEY_VALUE_HEADS * HEAD_SIZE) + EPS)
    for b in range(BLOCKS_HERE):
        norm_keys(b + HALO_BLOCKS, k_scale[b : b + 1])
    load_g.wait()

    def order(s):
        return jnp.where(s < 3, s + 4, jnp.where(s == 3, 3, jnp.where(s < 7, s - 4, 7)))

    def inner_copies(b):
        return [
            remote(
                inner.at[b], inner_all.at[head, b],
                inner_send.at[r - 1, b], inner_recv.at[r - 1, b], head=at_head(r),
            )
            for r in range(1, 4)
        ]

    def finish_queries(b):
        rows = block_rows(b)
        for copy in inner_copies(b):
            copy.wait_recv()
        summed = inner_all[0, b] + inner_all[1, b] + inner_all[2, b] + inner_all[3, b]
        mean = column(summed[0:1] / (QUERY_HEADS * HEAD_SIZE))
        scale = q_col[rows]
        for t in range(HEADS):
            unit = q_raw[rows, cols(t)].astype(F32) * scale
            qgrad[rows, cols(t)] = (scale * (u_all[rows, cols(t)] - unit * mean)).astype(BF16)

    def attend(b, biases, qn):
        rows = block_rows(b)
        window = pl.ds(pl.multiple_of(b * BLOCK, BLOCK), WINDOW)
        lower = tri[...] > 0.5
        scale = q_col[rows]

        def products_in(g, h):
            queries = jnp.concatenate([qn[:, cols(h + n)] for n in range(PAIR)], axis=0)
            grads = jnp.concatenate([go[rows, cols(h + n)] for n in range(PAIR)], axis=0)
            scores = dot(kn[window, cols(g)], queries, 1, 1)
            dweights = dot(vals[window, cols(g)], grads, 1, 1)
            return queries, grads, scores, dweights

        def fold(tiles, bias):
            tiles = [tiles[c * BLOCK : (c + 1) * BLOCK] for c in range(WINDOW_BLOCKS)]
            return [jnp.where(lower, tiles[-1], tiles[0] + bias)] + tiles[1:-1]

        def unfold(tiles):
            low = [tile.astype(BF16) for tile in tiles]
            return jnp.concatenate([low[0] * far[...]] + low[1:] + [low[0] * near[...]], axis=0)

        def softmax(scores, dweights):
            parts = fold(scores, biases[0])
            dparts = fold(dweights, 0.0)
            shifts = [0.0] + biases[1:-1]
            top = None
            for part, shift in zip(parts, shifts):
                here = jnp.max(part, axis=0, keepdims=True) + shift
                top = here if top is None else jnp.maximum(top, here)
            top = top * SCALE_LOG2
            expo = [
                jnp.exp2(part * SCALE_LOG2 - (top - shift)) for part, shift in zip(parts, shifts)
            ]
            inverse = 1.0 / sum(jnp.sum(e, axis=0, keepdims=True) for e in expo)
            weights = [e * inverse for e in expo]
            delta = sum(
                jnp.sum(w * d, axis=0, keepdims=True) for w, d in zip(weights, dparts)
            )
            dscores = [w * (d - delta) for w, d in zip(weights, dparts)]
            return unfold(weights), unfold(dscores)

        def products_out(g, h, queries, grads, weights_low, dscores_low):
            gc = cols(g)
            out_t = dot(v_t[gc, window], weights_low, 1, 0)
            dquery_t = dot(k_t[gc, window], dscores_low, 1, 0)
            dv[window, gc] += dot(weights_low, grads, 1, 0)
            dk[window, gc] += dot(dscores_low, queries, 1, 0)
            product = None
            for n in range(PAIR):
                hc = cols(h + n)
                att[rows, hc] = out_t[:, cols(n)].T.astype(BF16)
                dquery = dquery_t[:, cols(n)].T * SCALE
                onto = dquery * (q_raw[rows, hc].astype(F32) * scale)
                q_acc[:, hc] += eight(onto)
                gain = q_gain[:, hc]
                u_all[rows, hc] = dquery * gain
                product = onto * gain if product is None else product + onto * gain
            return product

        units = [(h // GROUP, h) for h in range(0, HEADS, PAIR)]
        product = None
        ahead = products_in(*units[0])
        for n, unit in enumerate(units):
            queries, grads, scores, dweights = ahead
            if n + 1 < len(units):
                ahead = products_in(*units[n + 1])
            low = softmax(scores, dweights)
            part = products_out(*unit, queries, grads, *low)
            product = part if product is None else product + part
        return product

    def back_copies(b):
        rows = block_rows(b)
        return [
            remote(back_k.at[rows], got_k.at[rows], back_send.at[0, b], back_recv.at[0, b], ctx=prv),
            remote(back_v.at[rows], got_v.at[rows], back_send.at[1, b], back_recv.at[1, b], ctx=prv),
        ]

    def send_back(b, start=True):
        rows = block_rows(b)
        scale = k_col[rows]
        product = None
        for t in range(GROUPS):
            dkey = dk[rows, cols(t)] * SCALE
            onto = dkey * (k_raw[rows, cols(t)].astype(F32) * scale)
            k_acc[:, cols(t)] += eight(onto)
            back_k[rows, cols(t)] = dkey.astype(BF16)
            back_v[rows, cols(t)] = dv[rows, cols(t)].astype(BF16)
            gain = k_gain[:, cols(t)]
            product = onto * gain if product is None else product + onto * gain
        if start:
            for copy in back_copies(b):
                copy.start()
        hin[pl.ds(b, 1), :] = row_sums(product)

    def exchange(src, dst, send, recv):
        return [
            remote(src, dst.at[head], send.at[r - 1], recv.at[r - 1], head=at_head(r))
            for r in range(1, 4)
        ]

    hin_copies = exchange(hin, hin_all, hin_send, hin_recv)

    def norm_queries(b, slot):
        rows = block_rows(b)
        scale = q_col[rows]
        for t in range(HEADS):
            unit = q_raw[rows, cols(t)].astype(F32) * scale
            qn[slot, :, cols(t)] = (unit * q_gain[:, cols(t)]).astype(BF16)

    def take_halo(n):
        for copy in halo_copies(n):
            copy.wait_recv()
        halo_scale = lax.rsqrt(halo_stat[...] / (KEY_VALUE_HEADS * HEAD_SIZE) + EPS)
        norm_keys(n, halo_scale[n + HALO_BLOCKS : n + HALO_BLOCKS + 1])
        turn_values(n, 0)

    def work(s):
        b = order(s)
        here = ctx * BLOCKS_HERE + b
        doc = docs[here]
        biases = []
        for c in range(WINDOW_BLOCKS):
            there = here - HALO_BLOCKS + c
            same = (docs[jnp.maximum(there, 0)] == doc) & (there >= 0)
            biases.append(jnp.where(same, 0.0, NEGATIVE))
        product = attend(b, biases, qn.at[s % 2])
        norm_queries(order(s + 1), (s + 1) % 2)
        tile = jnp.broadcast_to(row_sums(product), (8, 128))
        inner[b] = tile
        inner_all[head, b] = tile
        for copy in inner_copies(b):
            copy.start()

    def early(s, _):
        @pl.when(s == 3)
        def _():
            relay.wait_recv()
            take_halo(3)

        work(s)
        return 0

    def late(s, _):
        finish_queries(order(s - 4))
        work(s)

        @pl.when(s < 7)
        def _():
            send_back(s - 4)

        @pl.when(s == 6)
        def _():
            send_back(3, start=False)
            hin_all[head] = hin[...]
            for copy in hin_copies:
                copy.start()

        return 0

    hin[...] = jnp.zeros_like(hin)
    norm_queries(order(0), 0)
    lax.fori_loop(0, 4, early, 0)
    for n in range(3):
        take_halo(n)
    lax.fori_loop(4, BLOCKS_HERE, late, 0)

    for b in range(BLOCKS_HERE):
        rows = slice(HALO + b * BLOCK, HALO + (b + 1) * BLOCK)
        scale = k_col[rows]
        product = None
        for t in range(GROUPS):
            onto = dk[rows, cols(t)] * SCALE * (k_raw[rows, cols(t)].astype(F32) * scale)
            k_acc[:, cols(t)] += eight(onto)
            gain = k_gain[:, cols(t)]
            product = onto * gain if product is None else product + onto * gain
        products[b] = product

    for t in range(HEADS):
        gains[t : t + 1] = jnp.sum(q_acc[:, cols(t)], axis=0, keepdims=True)
    for t in range(GROUPS):
        gains[HEADS + t : HEADS + t + 1] = jnp.sum(k_acc[:, cols(t)], axis=0, keepdims=True)
    gains[HEADS + GROUPS :] = jnp.zeros((GAIN_ROWS - HEADS - GROUPS, 128), F32)
    x_copies = [
        remote(gains, gains_x.at[x], gain_send.at[r - 1], gain_recv.at[r - 1], ctx=at_x(r))
        for r in range(1, 4)
    ]
    for copy in x_copies:
        copy.start()
    gains_x[x] = gains[...]
    for b in range(BLOCKS_HERE):
        kin[b : b + 1] = row_sums(products[b])
    kin_copies = exchange(kin, kin_all, kin_send, kin_recv)
    for copy in kin_copies:
        copy.start()
    kin_all[head] = kin[...]

    for copy in hin_copies:
        copy.wait_recv()
    hin_sum[...] = hin_all[0] + hin_all[1] + hin_all[2] + hin_all[3]
    hin_back = remote(hin_sum, hin_got, hin_send.at[3], hin_recv.at[3], ctx=prv)
    hin_back.start()

    last_k, last_v = back_copies(HALO_BLOCKS - 1)
    last_k.start()
    for copy in x_copies:
        copy.wait_recv()
    gains_zy[zy] = gains_x[0] + gains_x[1] + gains_x[2] + gains_x[3]
    zy_copies = [
        remote(
            gains_zy.at[zy], gains_zy.at[zy], gain_send.at[r + 2], gain_recv.at[r + 2], ctx=at_zy(r)
        )
        for r in range(1, 8)
    ]
    for copy in zy_copies:
        copy.start()
    last_v.start()

    def finish_later(s, _):
        finish_queries(order(s))
        return 0

    lax.fori_loop(4, BLOCKS_HERE, finish_later, 0)

    for n in range(HALO_BLOCKS):
        for copy in back_copies(n):
            copy.wait_recv()
    split = TOKENS - HALO
    vgrad[0:split] = dv[HALO : HALO + split].astype(BF16)
    vgrad[split:] = (dv[HALO + split :] + got_v[...].astype(F32)).astype(BF16)

    for copy in kin_copies:
        copy.wait_recv()
    hin_back.wait_recv()
    kin_total = kin_all[0] + kin_all[1] + kin_all[2] + kin_all[3]
    got_total = hin_got[...]
    for b in range(BLOCKS_HERE):
        there = slice(b * BLOCK, (b + 1) * BLOCK)
        rows = slice(HALO + b * BLOCK, HALO + (b + 1) * BLOCK)
        row = kin_total[b : b + 1]
        n = b - (BLOCKS_HERE - HALO_BLOCKS)
        if n >= 0:
            row = row + got_total[n : n + 1]
        mean = column(row / (KEY_VALUE_HEADS * HEAD_SIZE))
        scale = k_col[rows]
        for t in range(GROUPS):
            dkey = dk[rows, cols(t)] * SCALE
            if n >= 0:
                dkey = dkey + got_k[n * BLOCK : (n + 1) * BLOCK, cols(t)].astype(F32)
            unit = k_raw[rows, cols(t)].astype(F32) * scale
            grad = scale * (dkey * k_gain[:, cols(t)] - unit * mean)
            kgrad[there, cols(t)] = grad.astype(BF16)

    for copy in zy_copies:
        copy.wait_recv()
    summed = gains_zy[0]
    for n in range(1, 8):
        summed = summed + gains_zy[n]
    for t in range(HEADS):
        qgain_out[:, cols(t)] = summed[t : t + 1]
    for t in range(GROUPS):
        kgain_out[:, cols(t)] = summed[HEADS + t : HEADS + t + 1]

    for copy in (
        [relay] + stat_copies + hin_copies + [hin_back] + kin_copies + x_copies + zy_copies
    ):
        copy.wait_send()
    for n in range(HALO_BLOCKS):
        for copy in halo_copies(n) + back_copies(n):
            copy.wait_send()

    def drain(b, _):
        for copy in inner_copies(b):
            copy.wait_send()
        return 0

    lax.fori_loop(0, BLOCKS_HERE, drain, 0)


def write(*refs):
    *pairs, sem = refs
    half = len(pairs) // 2
    copies = [
        pltpu.make_async_copy(src, dst, sem.at[n])
        for n, (src, dst) in enumerate(zip(pairs[:half], pairs[half:]))
    ]
    for copy in copies:
        copy.start()
    for copy in copies:
        copy.wait()


def local(query_raw, key_raw, values, output_gradient, query_gain, key_norm_gain, block_docs):
    hbm = pl.BlockSpec(memory_space=pltpu.HBM)
    vmem = pl.BlockSpec(memory_space=pltpu.VMEM)
    smem = pl.BlockSpec(memory_space=pltpu.SMEM)
    sems = pltpu.SemaphoreType.DMA
    stat = pltpu.VMEM((8, 128), F32)
    stats = pltpu.VMEM((HEAD_PEERS, 8, 128), F32)
    gain = pltpu.VMEM((GAIN_ROWS, 128), F32)
    scratch = [
        pltpu.VMEM((TOKENS, QCOLS), BF16),
        pltpu.VMEM((TOKENS, QCOLS), BF16),
        pltpu.VMEM((TOKENS, QCOLS), F32),
        pltpu.VMEM((2, BLOCK, QCOLS), BF16),
        pltpu.VMEM((EXT, KCOLS), BF16),
        pltpu.VMEM((EXT, KCOLS), BF16),
        pltpu.VMEM((EXT, KCOLS), BF16),
        pltpu.VMEM((KCOLS, EXT), BF16),
        pltpu.VMEM((KCOLS, EXT), BF16),
        pltpu.VMEM((EXT, KCOLS), F32),
        pltpu.VMEM((EXT, KCOLS), F32),
        pltpu.VMEM((HALO, KCOLS), BF16),
        pltpu.VMEM((HALO, KCOLS), BF16),
        pltpu.VMEM((HALO, KCOLS), BF16),
        pltpu.VMEM((HALO, KCOLS), BF16),
        pltpu.VMEM((TOKENS, 128), F32),
        pltpu.VMEM((EXT, 128), F32),
        pltpu.VMEM((BLOCK, PAIR * BLOCK), F32),
        pltpu.VMEM((BLOCK, PAIR * BLOCK), BF16),
        pltpu.VMEM((BLOCK, PAIR * BLOCK), BF16),
        pltpu.VMEM((16, 128), F32),
        pltpu.VMEM((HEAD_PEERS, 16, 128), F32),
        stat,
        stat,
        pltpu.VMEM((BLOCKS_HERE, 8, 128), F32),
        pltpu.VMEM((HEAD_PEERS, BLOCKS_HERE, 8, 128), F32),
        stat,
        stats,
        stat,
        stats,
        stat,
        stat,
        pltpu.VMEM((8, QCOLS), F32),
        pltpu.VMEM((8, KCOLS), F32),
        pltpu.VMEM((BLOCKS_HERE, 128, 128), F32),
        gain,
        pltpu.VMEM((4, GAIN_ROWS, 128), F32),
        pltpu.VMEM((8, GAIN_ROWS, 128), F32),
        sems((3 + QUERY_PIECES,)),
        sems((9,)),
        sems((9,)),
        sems((3,)),
        sems((3,)),
        sems((3, BLOCKS_HERE)),
        sems((3, BLOCKS_HERE)),
        sems((2, HALO_BLOCKS)),
        sems((2, HALO_BLOCKS)),
        sems((3,)),
        sems((3,)),
        sems((4,)),
        sems((4,)),
        sems((10,)),
        sems((10,)),
    ]
    shapes = [
        ((TOKENS, QCOLS), BF16),
        ((TOKENS, QCOLS), BF16),
        ((TOKENS, KCOLS), BF16),
        ((TOKENS, KCOLS), BF16),
        ((1, QCOLS), F32),
        ((1, KCOLS), F32),
    ]
    held = pl.pallas_call(
        kernel,
        out_shape=[pltpu.VMEM(*shape) for shape in shapes],
        in_specs=[hbm] * 4 + [vmem] * 2 + [smem],
        out_specs=[vmem] * 6,
        scratch_shapes=scratch,
        compiler_params=pltpu.CompilerParams(
            collective_id=0, has_side_effects=True, vmem_limit_bytes=56 * 2**20
        ),
        cost_estimate=pl.CostEstimate(
            flops=8_000_000_000, bytes_accessed=10_000_000, transcendentals=5_000_000
        ),
    )(
        query_raw, key_raw, values, output_gradient,
        query_gain.reshape(1, QCOLS), key_norm_gain.reshape(1, KCOLS), block_docs,
    )
    outs = pl.pallas_call(
        write,
        out_shape=[jax.ShapeDtypeStruct(*shape) for shape in shapes],
        in_specs=[vmem] * 6,
        out_specs=[hbm] * 6,
        scratch_shapes=[sems((6,))],
        compiler_params=pltpu.CompilerParams(vmem_limit_bytes=16 * 2**20),
    )(*[pltpu.with_memory_space_constraint(x, pltpu.VMEM) for x in held])
    return (*outs[:4], outs[4].reshape(QCOLS), outs[5].reshape(KCOLS))


def solution(mesh):
    placed = (
        P("ctx", "head"),
        P("ctx", "head"),
        P("ctx", "head"),
        P("ctx", "head"),
        P("head"),
        P("head"),
        P(),
    )
    return jax.shard_map(
        local,
        mesh=mesh,
        in_specs=placed,
        out_specs=(
            P("ctx", "head"),
            P("ctx", "head"),
            P("ctx", "head"),
            P("ctx", "head"),
            P("head"),
            P("head"),
        ),
        check_vma=False,
    )
```

```python
import jax
import jax.numpy as jnp
from jax import lax
from jax.experimental import pallas as pl
from jax.experimental.pallas import tpu as pltpu
from jax.sharding import PartitionSpec as P

QUERY_HEADS = 32
KEY_VALUE_HEADS = 8
HEAD_SIZE = 128
WINDOW_REACH = 512
BLOCK = 128
EPS = 1e-06
NEGATIVE = -1e30
SCALE = HEAD_SIZE ** (-0.5)
SCALE_LOG2 = SCALE * 1.4426950408889634

F32 = jnp.float32
BF16 = jnp.bfloat16
MESH = pl.DeviceIdType.MESH

TOKENS = 1024
BLOCKS_HERE = TOKENS // BLOCK
HALO = WINDOW_REACH
HALO_BLOCKS = HALO // BLOCK
WINDOW_BLOCKS = HALO_BLOCKS + 1
WINDOW = WINDOW_BLOCKS * BLOCK
EXT = HALO + TOKENS
GROUPS = 2
GROUP = 4
PAIR = 2
QUERY_PIECES = 4
HEADS = GROUPS * GROUP
QCOLS = HEADS * HEAD_SIZE
KCOLS = GROUPS * HEAD_SIZE
HEAD_PEERS = 4
GAIN_ROWS = 16


def dot(a, b, ca, cb):
    return lax.dot_general(a, b, (((ca,), (cb,)), ((), ())), preferred_element_type=F32)


def block_rows(b):
    return pl.ds(pl.multiple_of(b * BLOCK, BLOCK), BLOCK)


def cols(t):
    return slice(t * 128, (t + 1) * 128)


def column(row):
    return jnp.broadcast_to(row, (128, 128)).T


def row_sums(tile):
    return jnp.sum(tile.T, axis=0, keepdims=True)


def eight(tile):
    return jnp.sum(tile.reshape(16, 8, tile.shape[1]), axis=0)


def kernel(
    q_in, k_in, v_in, g_in, q_gain_in, k_gain_in, docs_in,
    att, qgrad, kgrad, vgrad, qgain_out, kgain_out,
    q_gain, k_gain, docs,
    q_raw, go, u_all, qn,
    k_raw, vals, kn, k_t, v_t, dk, dv,
    back_k, back_v, got_k, got_v,
    q_col, k_col, tri, near, far,
    stat, stat_all, k_stat, halo_stat,
    inner, inner_all, kin, kin_all, hin, hin_all, hin_sum, hin_got,
    q_acc, k_acc, products, gains, gains_x, gains_zy,
    load_sem, halo_send, halo_recv, stat_send, stat_recv,
    inner_send, inner_recv, back_send, back_recv, kin_send, kin_recv,
    hin_send, hin_recv, gain_send, gain_recv,
):
    ctx = lax.axis_index("ctx")
    head = lax.axis_index("head")
    x = ctx % 4
    z = (ctx // 4) % 4
    y = ctx // 16
    nxt = (ctx + 1) % 32
    prv = (ctx + 31) % 32

    def at_x(r):
        return (y * 4 + z) * 4 + (x + r) % 4

    zy = y * 4 + z

    def at_zy(r):
        return ((zy + r) % 8) * 4 + x

    def at_head(r):
        return (head + r) % HEAD_PEERS

    def remote(src, dst, send, recv, **where):
        return pltpu.make_async_remote_copy(
            src_ref=src, dst_ref=dst, send_sem=send, recv_sem=recv,
            device_id=where, device_id_type=MESH,
        )

    own = pl.ds(HALO, TOKENS)
    load_k = pltpu.make_async_copy(k_in, k_raw.at[own], load_sem.at[0])
    load_v = pltpu.make_async_copy(v_in, vals.at[own], load_sem.at[1])
    load_g = pltpu.make_async_copy(g_in, go, load_sem.at[2])
    load_q = []
    for n in range(QUERY_PIECES):
        rows = pl.ds(n * (TOKENS // QUERY_PIECES), TOKENS // QUERY_PIECES)
        load_q.append(pltpu.make_async_copy(q_in.at[rows], q_raw.at[rows], load_sem.at[3 + n]))
    for copy in load_q:
        copy.start()
    load_k.start()
    load_small = [
        pltpu.make_async_copy(q_gain_in, q_gain, load_sem.at[3 + QUERY_PIECES]),
        pltpu.make_async_copy(k_gain_in, k_gain, load_sem.at[4 + QUERY_PIECES]),
        pltpu.make_async_copy(docs_in, docs, load_sem.at[5 + QUERY_PIECES]),
    ]
    for copy in load_small:
        copy.start()

    barrier = pltpu.get_barrier_semaphore()
    for r in range(1, 4):
        pl.semaphore_signal(barrier, inc=1, device_id={"head": at_head(r)}, device_id_type=MESH)
        pl.semaphore_signal(barrier, inc=1, device_id={"ctx": at_x(r)}, device_id_type=MESH)
    for r in range(1, 8):
        pl.semaphore_signal(barrier, inc=1, device_id={"ctx": at_zy(r)}, device_id_type=MESH)
    for other in (nxt, prv):
        pl.semaphore_signal(barrier, inc=1, device_id={"ctx": other}, device_id_type=MESH)

    def halo_copies(n):
        there = pl.ds(TOKENS - HALO + n * BLOCK, BLOCK)
        here = pl.ds(n * BLOCK, BLOCK)
        return [
            remote(k_in.at[there], k_raw.at[here], halo_send.at[n], halo_recv.at[n], ctx=nxt),
            remote(
                v_in.at[there], vals.at[here], halo_send.at[4 + n], halo_recv.at[4 + n], ctx=nxt
            ),
        ]

    def send_halo(*chunks):
        for n in chunks:
            for copy in halo_copies(n):
                copy.start()

    for b in range(BLOCKS_HERE):
        if b % (BLOCKS_HERE // QUERY_PIECES) == 0:
            load_q[b * QUERY_PIECES // BLOCKS_HERE].wait()
        rows = slice(b * BLOCK, (b + 1) * BLOCK)
        total = None
        for t in range(HEADS):
            part = q_raw[rows, cols(t)].astype(F32)
            total = part * part if total is None else total + part * part
        stat[b : b + 1] = row_sums(total)
    load_k.wait()
    load_v.start()
    load_g.start()
    for b in range(BLOCKS_HERE):
        rows = slice(HALO + b * BLOCK, HALO + (b + 1) * BLOCK)
        total = None
        for t in range(GROUPS):
            part = k_raw[rows, cols(t)].astype(F32)
            total = part * part if total is None else total + part * part
        stat[b + 8 : b + 9] = row_sums(total)

    pl.semaphore_wait(barrier, 15)
    stat_copies = [
        remote(stat, stat_all.at[head], stat_send.at[r - 1], stat_recv.at[r - 1], head=at_head(r))
        for r in range(1, 4)
    ]
    for copy in stat_copies:
        copy.start()
    stat_all[head] = stat[...]

    send_halo(3)

    key_at = lax.broadcasted_iota(jnp.int32, (BLOCK, BLOCK), 0)
    query_at = lax.broadcasted_iota(jnp.int32, (BLOCK, BLOCK), 1)
    lower = jnp.where(key_at <= query_at, 1.0, 0.0)
    tri[...] = jnp.concatenate([lower] * PAIR, axis=1)
    near[...] = jnp.concatenate([lower] * PAIR, axis=1).astype(BF16)
    far[...] = (1.0 - jnp.concatenate([lower] * PAIR, axis=1)).astype(BF16)
    dk[...] = jnp.zeros_like(dk)
    dv[...] = jnp.zeros_like(dv)
    q_acc[...] = jnp.zeros_like(q_acc)
    k_acc[...] = jnp.zeros_like(k_acc)
    load_v.wait()

    def turn_values(b, _):
        rows = block_rows(b)
        for t in range(GROUPS):
            v_t[cols(t), rows] = vals[rows, cols(t)].T
        return 0

    lax.fori_loop(HALO_BLOCKS, EXT // BLOCK, turn_values, 0)

    for copy in stat_copies:
        copy.wait_recv()
    total = stat_all[0] + stat_all[1] + stat_all[2] + stat_all[3]
    k_stat[...] = total[8:16]
    relay = remote(k_stat, halo_stat, halo_send.at[8], halo_recv.at[8], ctx=nxt)
    relay.start()
    send_halo(2, 1, 0)

    q_scale = lax.rsqrt(total[0:8] / (QUERY_HEADS * HEAD_SIZE) + EPS)
    for b in range(BLOCKS_HERE):
        q_col[b * BLOCK : (b + 1) * BLOCK] = column(q_scale[b : b + 1])

    def norm_keys(b, scale_row):
        rows = slice(b * BLOCK, (b + 1) * BLOCK)
        scale = column(scale_row)
        k_col[rows] = scale
        for t in range(GROUPS):
            unit = k_raw[rows, cols(t)].astype(F32) * scale
            normed = (unit * k_gain[:, cols(t)]).astype(BF16)
            kn[rows, cols(t)] = normed
            k_t[cols(t), rows] = normed.T

    for copy in load_small:
        copy.wait()
    k_scale = lax.rsqrt(total[8:16] / (KEY_VALUE_HEADS * HEAD_SIZE) + EPS)
    for b in range(BLOCKS_HERE):
        norm_keys(b + HALO_BLOCKS, k_scale[b : b + 1])
    load_g.wait()

    def order(s):
        return jnp.where(s < 3, s + 4, jnp.where(s == 3, 3, jnp.where(s < 7, s - 4, 7)))

    def inner_copies(b):
        return [
            remote(
                inner.at[b], inner_all.at[head, b],
                inner_send.at[r - 1, b], inner_recv.at[r - 1, b], head=at_head(r),
            )
            for r in range(1, 4)
        ]

    def finish_queries(b):
        rows = block_rows(b)
        for copy in inner_copies(b):
            copy.wait_recv()
        summed = inner_all[0, b] + inner_all[1, b] + inner_all[2, b] + inner_all[3, b]
        mean = column(summed[0:1] / (QUERY_HEADS * HEAD_SIZE))
        scale = q_col[rows]
        for t in range(HEADS):
            unit = q_raw[rows, cols(t)].astype(F32) * scale
            qgrad[rows, cols(t)] = (scale * (u_all[rows, cols(t)] - unit * mean)).astype(BF16)

    def attend(b, biases, qn):
        rows = block_rows(b)
        window = pl.ds(pl.multiple_of(b * BLOCK, BLOCK), WINDOW)
        lower = tri[...] > 0.5
        scale = q_col[rows]

        def products_in(g, h):
            queries = jnp.concatenate([qn[:, cols(h + n)] for n in range(PAIR)], axis=0)
            grads = jnp.concatenate([go[rows, cols(h + n)] for n in range(PAIR)], axis=0)
            scores = dot(kn[window, cols(g)], queries, 1, 1)
            dweights = dot(vals[window, cols(g)], grads, 1, 1)
            return queries, grads, scores, dweights

        def fold(tiles, bias):
            tiles = [tiles[c * BLOCK : (c + 1) * BLOCK] for c in range(WINDOW_BLOCKS)]
            return [jnp.where(lower, tiles[-1], tiles[0] + bias)] + tiles[1:-1]

        def unfold(tiles):
            low = [tile.astype(BF16) for tile in tiles]
            return jnp.concatenate([low[0] * far[...]] + low[1:] + [low[0] * near[...]], axis=0)

        def softmax(scores, dweights):
            parts = fold(scores, biases[0])
            dparts = fold(dweights, 0.0)
            shifts = [0.0] + biases[1:-1]
            top = None
            for part, shift in zip(parts, shifts):
                here = jnp.max(part, axis=0, keepdims=True) + shift
                top = here if top is None else jnp.maximum(top, here)
            top = top * SCALE_LOG2
            expo = [
                jnp.exp2(part * SCALE_LOG2 - (top - shift)) for part, shift in zip(parts, shifts)
            ]
            inverse = 1.0 / sum(jnp.sum(e, axis=0, keepdims=True) for e in expo)
            weights = [e * inverse for e in expo]
            delta = sum(
                jnp.sum(w * d, axis=0, keepdims=True) for w, d in zip(weights, dparts)
            )
            dscores = [w * (d - delta) for w, d in zip(weights, dparts)]
            return unfold(weights), unfold(dscores)

        def products_out(g, h, queries, grads, weights_low, dscores_low):
            gc = cols(g)
            out_t = dot(v_t[gc, window], weights_low, 1, 0)
            dquery_t = dot(k_t[gc, window], dscores_low, 1, 0)
            dv[window, gc] += dot(weights_low, grads, 1, 0)
            dk[window, gc] += dot(dscores_low, queries, 1, 0)
            product = None
            for n in range(PAIR):
                hc = cols(h + n)
                att[rows, hc] = out_t[:, cols(n)].T.astype(BF16)
                dquery = dquery_t[:, cols(n)].T * SCALE
                onto = dquery * (q_raw[rows, hc].astype(F32) * scale)
                q_acc[:, hc] += eight(onto)
                gain = q_gain[:, hc]
                u_all[rows, hc] = dquery * gain
                product = onto * gain if product is None else product + onto * gain
            return product

        units = [(h // GROUP, h) for h in range(0, HEADS, PAIR)]
        product = None
        ahead = products_in(*units[0])
        for n, unit in enumerate(units):
            queries, grads, scores, dweights = ahead
            if n + 1 < len(units):
                ahead = products_in(*units[n + 1])
            low = softmax(scores, dweights)
            part = products_out(*unit, queries, grads, *low)
            product = part if product is None else product + part
        return product

    def back_copies(b):
        rows = block_rows(b)
        return [
            remote(back_k.at[rows], got_k.at[rows], back_send.at[0, b], back_recv.at[0, b], ctx=prv),
            remote(back_v.at[rows], got_v.at[rows], back_send.at[1, b], back_recv.at[1, b], ctx=prv),
        ]

    def send_back(b, start=True):
        rows = block_rows(b)
        scale = k_col[rows]
        product = None
        for t in range(GROUPS):
            dkey = dk[rows, cols(t)] * SCALE
            onto = dkey * (k_raw[rows, cols(t)].astype(F32) * scale)
            k_acc[:, cols(t)] += eight(onto)
            back_k[rows, cols(t)] = dkey.astype(BF16)
            back_v[rows, cols(t)] = dv[rows, cols(t)].astype(BF16)
            gain = k_gain[:, cols(t)]
            product = onto * gain if product is None else product + onto * gain
        if start:
            for copy in back_copies(b):
                copy.start()
        hin[pl.ds(b, 1), :] = row_sums(product)

    def exchange(src, dst, send, recv):
        return [
            remote(src, dst.at[head], send.at[r - 1], recv.at[r - 1], head=at_head(r))
            for r in range(1, 4)
        ]

    hin_copies = exchange(hin, hin_all, hin_send, hin_recv)

    def norm_queries(b, slot):
        rows = block_rows(b)
        scale = q_col[rows]
        for t in range(HEADS):
            unit = q_raw[rows, cols(t)].astype(F32) * scale
            qn[slot, :, cols(t)] = (unit * q_gain[:, cols(t)]).astype(BF16)

    def take_halo(n):
        for copy in halo_copies(n):
            copy.wait_recv()
        halo_scale = lax.rsqrt(halo_stat[...] / (KEY_VALUE_HEADS * HEAD_SIZE) + EPS)
        norm_keys(n, halo_scale[n + HALO_BLOCKS : n + HALO_BLOCKS + 1])
        turn_values(n, 0)

    def work(s):
        b = order(s)
        here = ctx * BLOCKS_HERE + b
        doc = docs[here]
        biases = []
        for c in range(WINDOW_BLOCKS):
            there = here - HALO_BLOCKS + c
            same = (docs[jnp.maximum(there, 0)] == doc) & (there >= 0)
            biases.append(jnp.where(same, 0.0, NEGATIVE))
        product = attend(b, biases, qn.at[s % 2])
        norm_queries(order(s + 1), (s + 1) % 2)
        tile = jnp.broadcast_to(row_sums(product), (8, 128))
        inner[b] = tile
        inner_all[head, b] = tile
        for copy in inner_copies(b):
            copy.start()

    def early(s, _):
        @pl.when(s == 3)
        def _():
            relay.wait_recv()
            take_halo(3)

        work(s)
        return 0

    def late(s, _):
        finish_queries(order(s - 4))
        work(s)

        @pl.when(s < 7)
        def _():
            send_back(s - 4)

        @pl.when(s == 6)
        def _():
            send_back(3, start=False)
            hin_all[head] = hin[...]
            for copy in hin_copies:
                copy.start()

        return 0

    hin[...] = jnp.zeros_like(hin)
    norm_queries(order(0), 0)
    lax.fori_loop(0, 4, early, 0)
    for n in range(3):
        take_halo(n)
    lax.fori_loop(4, BLOCKS_HERE, late, 0)

    for b in range(BLOCKS_HERE):
        rows = slice(HALO + b * BLOCK, HALO + (b + 1) * BLOCK)
        scale = k_col[rows]
        product = None
        for t in range(GROUPS):
            onto = dk[rows, cols(t)] * SCALE * (k_raw[rows, cols(t)].astype(F32) * scale)
            k_acc[:, cols(t)] += eight(onto)
            gain = k_gain[:, cols(t)]
            product = onto * gain if product is None else product + onto * gain
        products[b] = product

    for t in range(HEADS):
        gains[t : t + 1] = jnp.sum(q_acc[:, cols(t)], axis=0, keepdims=True)
    for t in range(GROUPS):
        gains[HEADS + t : HEADS + t + 1] = jnp.sum(k_acc[:, cols(t)], axis=0, keepdims=True)
    gains[HEADS + GROUPS :] = jnp.zeros((GAIN_ROWS - HEADS - GROUPS, 128), F32)
    x_copies = [
        remote(gains, gains_x.at[x], gain_send.at[r - 1], gain_recv.at[r - 1], ctx=at_x(r))
        for r in range(1, 4)
    ]
    for copy in x_copies:
        copy.start()
    gains_x[x] = gains[...]
    for b in range(BLOCKS_HERE):
        kin[b : b + 1] = row_sums(products[b])
    kin_copies = exchange(kin, kin_all, kin_send, kin_recv)
    for copy in kin_copies:
        copy.start()
    kin_all[head] = kin[...]

    for copy in hin_copies:
        copy.wait_recv()
    hin_sum[...] = hin_all[0] + hin_all[1] + hin_all[2] + hin_all[3]
    hin_back = remote(hin_sum, hin_got, hin_send.at[3], hin_recv.at[3], ctx=prv)
    hin_back.start()

    last_k, last_v = back_copies(HALO_BLOCKS - 1)
    last_k.start()
    for copy in x_copies:
        copy.wait_recv()
    gains_zy[zy] = gains_x[0] + gains_x[1] + gains_x[2] + gains_x[3]
    zy_copies = [
        remote(
            gains_zy.at[zy], gains_zy.at[zy], gain_send.at[r + 2], gain_recv.at[r + 2], ctx=at_zy(r)
        )
        for r in range(1, 8)
    ]
    for copy in zy_copies:
        copy.start()
    last_v.start()

    def finish_later(s, _):
        finish_queries(order(s))
        return 0

    lax.fori_loop(4, BLOCKS_HERE, finish_later, 0)

    for n in range(HALO_BLOCKS):
        for copy in back_copies(n):
            copy.wait_recv()
    split = TOKENS - HALO
    vgrad[0:split] = dv[HALO : HALO + split].astype(BF16)
    vgrad[split:] = (dv[HALO + split :] + got_v[...].astype(F32)).astype(BF16)

    for copy in kin_copies:
        copy.wait_recv()
    hin_back.wait_recv()
    kin_total = kin_all[0] + kin_all[1] + kin_all[2] + kin_all[3]
    got_total = hin_got[...]
    for b in range(BLOCKS_HERE):
        there = slice(b * BLOCK, (b + 1) * BLOCK)
        rows = slice(HALO + b * BLOCK, HALO + (b + 1) * BLOCK)
        row = kin_total[b : b + 1]
        n = b - (BLOCKS_HERE - HALO_BLOCKS)
        if n >= 0:
            row = row + got_total[n : n + 1]
        mean = column(row / (KEY_VALUE_HEADS * HEAD_SIZE))
        scale = k_col[rows]
        for t in range(GROUPS):
            dkey = dk[rows, cols(t)] * SCALE
            if n >= 0:
                dkey = dkey + got_k[n * BLOCK : (n + 1) * BLOCK, cols(t)].astype(F32)
            unit = k_raw[rows, cols(t)].astype(F32) * scale
            grad = scale * (dkey * k_gain[:, cols(t)] - unit * mean)
            kgrad[there, cols(t)] = grad.astype(BF16)

    for copy in zy_copies:
        copy.wait_recv()
    summed = gains_zy[0]
    for n in range(1, 8):
        summed = summed + gains_zy[n]
    for t in range(HEADS):
        qgain_out[:, cols(t)] = summed[t : t + 1]
    for t in range(GROUPS):
        kgain_out[:, cols(t)] = summed[HEADS + t : HEADS + t + 1]

    for copy in (
        [relay] + stat_copies + hin_copies + [hin_back] + kin_copies + x_copies + zy_copies
    ):
        copy.wait_send()
    for n in range(HALO_BLOCKS):
        for copy in halo_copies(n) + back_copies(n):
            copy.wait_send()

    def drain(b, _):
        for copy in inner_copies(b):
            copy.wait_send()
        return 0

    lax.fori_loop(0, BLOCKS_HERE, drain, 0)


def write(*refs):
    *pairs, sem = refs
    half = len(pairs) // 2
    copies = [
        pltpu.make_async_copy(src, dst, sem.at[n])
        for n, (src, dst) in enumerate(zip(pairs[:half], pairs[half:]))
    ]
    for copy in copies:
        copy.start()
    for copy in copies:
        copy.wait()


def local(query_raw, key_raw, values, output_gradient, query_gain, key_norm_gain, block_docs):
    hbm = pl.BlockSpec(memory_space=pltpu.HBM)
    vmem = pl.BlockSpec(memory_space=pltpu.VMEM)
    sems = pltpu.SemaphoreType.DMA
    stat = pltpu.VMEM((8, 128), F32)
    stats = pltpu.VMEM((HEAD_PEERS, 8, 128), F32)
    gain = pltpu.VMEM((GAIN_ROWS, 128), F32)
    scratch = [
        pltpu.VMEM((1, QCOLS), F32),
        pltpu.VMEM((1, KCOLS), F32),
        pltpu.SMEM((256,), jnp.int32),
        pltpu.VMEM((TOKENS, QCOLS), BF16),
        pltpu.VMEM((TOKENS, QCOLS), BF16),
        pltpu.VMEM((TOKENS, QCOLS), F32),
        pltpu.VMEM((2, BLOCK, QCOLS), BF16),
        pltpu.VMEM((EXT, KCOLS), BF16),
        pltpu.VMEM((EXT, KCOLS), BF16),
        pltpu.VMEM((EXT, KCOLS), BF16),
        pltpu.VMEM((KCOLS, EXT), BF16),
        pltpu.VMEM((KCOLS, EXT), BF16),
        pltpu.VMEM((EXT, KCOLS), F32),
        pltpu.VMEM((EXT, KCOLS), F32),
        pltpu.VMEM((HALO, KCOLS), BF16),
        pltpu.VMEM((HALO, KCOLS), BF16),
        pltpu.VMEM((HALO, KCOLS), BF16),
        pltpu.VMEM((HALO, KCOLS), BF16),
        pltpu.VMEM((TOKENS, 128), F32),
        pltpu.VMEM((EXT, 128), F32),
        pltpu.VMEM((BLOCK, PAIR * BLOCK), F32),
        pltpu.VMEM((BLOCK, PAIR * BLOCK), BF16),
        pltpu.VMEM((BLOCK, PAIR * BLOCK), BF16),
        pltpu.VMEM((16, 128), F32),
        pltpu.VMEM((HEAD_PEERS, 16, 128), F32),
        stat,
        stat,
        pltpu.VMEM((BLOCKS_HERE, 8, 128), F32),
        pltpu.VMEM((HEAD_PEERS, BLOCKS_HERE, 8, 128), F32),
        stat,
        stats,
        stat,
        stats,
        stat,
        stat,
        pltpu.VMEM((8, QCOLS), F32),
        pltpu.VMEM((8, KCOLS), F32),
        pltpu.VMEM((BLOCKS_HERE, 128, 128), F32),
        gain,
        pltpu.VMEM((4, GAIN_ROWS, 128), F32),
        pltpu.VMEM((8, GAIN_ROWS, 128), F32),
        sems((6 + QUERY_PIECES,)),
        sems((9,)),
        sems((9,)),
        sems((3,)),
        sems((3,)),
        sems((3, BLOCKS_HERE)),
        sems((3, BLOCKS_HERE)),
        sems((2, HALO_BLOCKS)),
        sems((2, HALO_BLOCKS)),
        sems((3,)),
        sems((3,)),
        sems((4,)),
        sems((4,)),
        sems((10,)),
        sems((10,)),
    ]
    shapes = [
        ((TOKENS, QCOLS), BF16),
        ((TOKENS, QCOLS), BF16),
        ((TOKENS, KCOLS), BF16),
        ((TOKENS, KCOLS), BF16),
        ((1, QCOLS), F32),
        ((1, KCOLS), F32),
    ]
    held = pl.pallas_call(
        kernel,
        out_shape=[pltpu.VMEM(*shape) for shape in shapes],
        in_specs=[hbm] * 7,
        out_specs=[vmem] * 6,
        scratch_shapes=scratch,
        compiler_params=pltpu.CompilerParams(
            collective_id=0, has_side_effects=True, vmem_limit_bytes=56 * 2**20
        ),
        cost_estimate=pl.CostEstimate(
            flops=8_000_000_000, bytes_accessed=10_000_000, transcendentals=5_000_000
        ),
    )(
        query_raw, key_raw, values, output_gradient,
        query_gain.reshape(1, QCOLS), key_norm_gain.reshape(1, KCOLS), block_docs,
    )
    outs = pl.pallas_call(
        write,
        out_shape=[jax.ShapeDtypeStruct(*shape) for shape in shapes],
        in_specs=[vmem] * 6,
        out_specs=[hbm] * 6,
        scratch_shapes=[sems((6,))],
        compiler_params=pltpu.CompilerParams(vmem_limit_bytes=16 * 2**20),
    )(*[pltpu.with_memory_space_constraint(x, pltpu.VMEM) for x in held])
    return (*outs[:4], outs[4].reshape(QCOLS), outs[5].reshape(KCOLS))


def solution(mesh):
    placed = (
        P("ctx", "head"),
        P("ctx", "head"),
        P("ctx", "head"),
        P("ctx", "head"),
        P("head"),
        P("head"),
        P(),
    )
    return jax.shard_map(
        local,
        mesh=mesh,
        in_specs=placed,
        out_specs=(
            P("ctx", "head"),
            P("ctx", "head"),
            P("ctx", "head"),
            P("ctx", "head"),
            P("head"),
            P("head"),
        ),
        check_vma=False,
    )
```

```python
import jax
import jax.numpy as jnp
from jax import lax
from jax.experimental import pallas as pl
from jax.experimental.pallas import tpu as pltpu
from jax.sharding import PartitionSpec as P

QUERY_HEADS = 32
KEY_VALUE_HEADS = 8
HEAD_SIZE = 128
WINDOW_REACH = 512
BLOCK = 128
EPS = 1e-06
NEGATIVE = -1e30
SCALE = HEAD_SIZE ** (-0.5)
SCALE_LOG2 = SCALE * 1.4426950408889634

F32 = jnp.float32
BF16 = jnp.bfloat16
MESH = pl.DeviceIdType.MESH

TOKENS = 1024
BLOCKS_HERE = TOKENS // BLOCK
HALO = WINDOW_REACH
HALO_BLOCKS = HALO // BLOCK
WINDOW_BLOCKS = HALO_BLOCKS + 1
WINDOW = WINDOW_BLOCKS * BLOCK
EXT = HALO + TOKENS
GROUPS = 2
GROUP = 4
PAIR = 2
QUERY_PIECES = 4
HEADS = GROUPS * GROUP
QCOLS = HEADS * HEAD_SIZE
KCOLS = GROUPS * HEAD_SIZE
HEAD_PEERS = 4
GAIN_ROWS = 16


def dot(a, b, ca, cb):
    return lax.dot_general(a, b, (((ca,), (cb,)), ((), ())), preferred_element_type=F32)


def block_rows(b):
    return pl.ds(pl.multiple_of(b * BLOCK, BLOCK), BLOCK)


def cols(t):
    return slice(t * 128, (t + 1) * 128)


def column(row):
    return jnp.broadcast_to(row, (128, 128)).T


def row_sums(tile):
    return jnp.sum(tile.T, axis=0, keepdims=True)


def eight(tile):
    return jnp.sum(tile.reshape(16, 8, tile.shape[1]), axis=0)


def kernel(
    q_in, k_in, v_in, g_in, q_gain_in, k_gain_in, docs_in,
    att, qgrad, kgrad, vgrad, qgain_out, kgain_out,
    q_gain, k_gain, docs,
    q_raw, go, u_all, qn,
    k_raw, vals, kn, k_t, v_t, dk, dv,
    back_k, back_v, got_k, got_v,
    q_col, k_col, tri, near, far,
    stat, stat_all, k_stat, halo_stat,
    inner, inner_all, kin, kin_all, hin, hin_all, hin_sum, hin_got,
    q_acc, k_acc, products, gains, gains_x, gains_zy,
    load_sem, halo_send, halo_recv, stat_send, stat_recv,
    inner_send, inner_recv, back_send, back_recv, kin_send, kin_recv,
    hin_send, hin_recv, gain_send, gain_recv,
):
    ctx = lax.axis_index("ctx")
    head = lax.axis_index("head")
    x = ctx % 4
    z = (ctx // 4) % 4
    y = ctx // 16
    nxt = (ctx + 1) % 32
    prv = (ctx + 31) % 32

    def at_x(r):
        return (y * 4 + z) * 4 + (x + r) % 4

    zy = y * 4 + z

    def at_zy(r):
        return ((zy + r) % 8) * 4 + x

    def at_head(r):
        return (head + r) % HEAD_PEERS

    def remote(src, dst, send, recv, **where):
        return pltpu.make_async_remote_copy(
            src_ref=src, dst_ref=dst, send_sem=send, recv_sem=recv,
            device_id=where, device_id_type=MESH,
        )

    own = pl.ds(HALO, TOKENS)
    load_k = pltpu.make_async_copy(k_in, k_raw.at[own], load_sem.at[0])
    load_v = pltpu.make_async_copy(v_in, vals.at[own], load_sem.at[1])
    load_g = pltpu.make_async_copy(g_in, go, load_sem.at[2])
    load_q = []
    for n in range(QUERY_PIECES):
        rows = pl.ds(n * (TOKENS // QUERY_PIECES), TOKENS // QUERY_PIECES)
        load_q.append(pltpu.make_async_copy(q_in.at[rows], q_raw.at[rows], load_sem.at[3 + n]))
    for copy in load_q:
        copy.start()
    load_k.start()
    load_small = [
        pltpu.make_async_copy(q_gain_in, q_gain, load_sem.at[3 + QUERY_PIECES]),
        pltpu.make_async_copy(k_gain_in, k_gain, load_sem.at[4 + QUERY_PIECES]),
        pltpu.make_async_copy(docs_in, docs, load_sem.at[5 + QUERY_PIECES]),
    ]
    for copy in load_small:
        copy.start()

    barrier = pltpu.get_barrier_semaphore()
    for r in range(1, 4):
        pl.semaphore_signal(barrier, inc=1, device_id={"head": at_head(r)}, device_id_type=MESH)
        pl.semaphore_signal(barrier, inc=1, device_id={"ctx": at_x(r)}, device_id_type=MESH)
    for r in range(1, 8):
        pl.semaphore_signal(barrier, inc=1, device_id={"ctx": at_zy(r)}, device_id_type=MESH)
    for other in (nxt, prv):
        pl.semaphore_signal(barrier, inc=1, device_id={"ctx": other}, device_id_type=MESH)

    def halo_copies(n):
        there = pl.ds(TOKENS - HALO + n * BLOCK, BLOCK)
        here = pl.ds(n * BLOCK, BLOCK)
        return [
            remote(k_in.at[there], k_raw.at[here], halo_send.at[n], halo_recv.at[n], ctx=nxt),
            remote(
                v_in.at[there], vals.at[here], halo_send.at[4 + n], halo_recv.at[4 + n], ctx=nxt
            ),
        ]

    def send_halo(*chunks):
        for n in chunks:
            for copy in halo_copies(n):
                copy.start()

    for b in range(BLOCKS_HERE):
        if b % (BLOCKS_HERE // QUERY_PIECES) == 0:
            load_q[b * QUERY_PIECES // BLOCKS_HERE].wait()
        rows = slice(b * BLOCK, (b + 1) * BLOCK)
        total = None
        for t in range(HEADS):
            part = q_raw[rows, cols(t)].astype(F32)
            total = part * part if total is None else total + part * part
        stat[b : b + 1] = row_sums(total)
    load_k.wait()
    load_v.start()
    load_g.start()
    for b in range(BLOCKS_HERE):
        rows = slice(HALO + b * BLOCK, HALO + (b + 1) * BLOCK)
        total = None
        for t in range(GROUPS):
            part = k_raw[rows, cols(t)].astype(F32)
            total = part * part if total is None else total + part * part
        stat[b + 8 : b + 9] = row_sums(total)

    pl.semaphore_wait(barrier, 15)
    stat_copies = [
        remote(stat, stat_all.at[head], stat_send.at[r - 1], stat_recv.at[r - 1], head=at_head(r))
        for r in range(1, 4)
    ]
    for copy in stat_copies:
        copy.start()
    stat_all[head] = stat[...]

    send_halo(3)

    key_at = lax.broadcasted_iota(jnp.int32, (BLOCK, BLOCK), 0)
    query_at = lax.broadcasted_iota(jnp.int32, (BLOCK, BLOCK), 1)
    lower = jnp.where(key_at <= query_at, 1.0, 0.0)
    tri[...] = jnp.concatenate([lower] * PAIR, axis=1)
    near[...] = jnp.concatenate([lower] * PAIR, axis=1).astype(BF16)
    far[...] = (1.0 - jnp.concatenate([lower] * PAIR, axis=1)).astype(BF16)
    dk[...] = jnp.zeros_like(dk)
    dv[...] = jnp.zeros_like(dv)
    q_acc[...] = jnp.zeros_like(q_acc)
    k_acc[...] = jnp.zeros_like(k_acc)
    load_v.wait()

    def turn_values(b, _):
        rows = block_rows(b)
        for t in range(GROUPS):
            v_t[cols(t), rows] = vals[rows, cols(t)].T
        return 0

    lax.fori_loop(HALO_BLOCKS, EXT // BLOCK, turn_values, 0)

    for copy in stat_copies:
        copy.wait_recv()
    total = stat_all[0] + stat_all[1] + stat_all[2] + stat_all[3]
    k_stat[...] = total[8:16]
    relay = remote(k_stat, halo_stat, halo_send.at[8], halo_recv.at[8], ctx=nxt)
    relay.start()
    send_halo(2, 1, 0)

    q_scale = lax.rsqrt(total[0:8] / (QUERY_HEADS * HEAD_SIZE) + EPS)
    for b in range(BLOCKS_HERE):
        q_col[b * BLOCK : (b + 1) * BLOCK] = column(q_scale[b : b + 1])

    def norm_keys(b, scale_row):
        rows = slice(b * BLOCK, (b + 1) * BLOCK)
        scale = column(scale_row)
        k_col[rows] = scale
        for t in range(GROUPS):
            unit = k_raw[rows, cols(t)].astype(F32) * scale
            normed = (unit * k_gain[:, cols(t)]).astype(BF16)
            kn[rows, cols(t)] = normed
            k_t[cols(t), rows] = normed.T

    for copy in load_small:
        copy.wait()
    k_scale = lax.rsqrt(total[8:16] / (KEY_VALUE_HEADS * HEAD_SIZE) + EPS)
    for b in range(BLOCKS_HERE):
        norm_keys(b + HALO_BLOCKS, k_scale[b : b + 1])
    load_g.wait()

    def order(s):
        return jnp.where(s < 3, s + 4, jnp.where(s == 3, 3, jnp.where(s < 7, s - 4, 7)))

    def inner_copies(b):
        return [
            remote(
                inner.at[b], inner_all.at[head, b],
                inner_send.at[r - 1, b], inner_recv.at[r - 1, b], head=at_head(r),
            )
            for r in range(1, 4)
        ]

    def finish_queries(b):
        rows = block_rows(b)
        for copy in inner_copies(b):
            copy.wait_recv()
        summed = inner_all[0, b] + inner_all[1, b] + inner_all[2, b] + inner_all[3, b]
        mean = column(summed[0:1] / (QUERY_HEADS * HEAD_SIZE))
        scale = q_col[rows]
        for t in range(HEADS):
            unit = q_raw[rows, cols(t)].astype(F32) * scale
            qgrad[rows, cols(t)] = (scale * (u_all[rows, cols(t)] - unit * mean)).astype(BF16)

    def attend(b, biases, qn):
        rows = block_rows(b)
        window = pl.ds(pl.multiple_of(b * BLOCK, BLOCK), WINDOW)
        lower = tri[...] > 0.5
        scale = q_col[rows]

        def products_in(g, h):
            queries = jnp.concatenate([qn[:, cols(h + n)] for n in range(PAIR)], axis=0)
            grads = jnp.concatenate([go[rows, cols(h + n)] for n in range(PAIR)], axis=0)
            scores = dot(kn[window, cols(g)], queries, 1, 1)
            dweights = dot(vals[window, cols(g)], grads, 1, 1)
            return queries, grads, scores, dweights

        def fold(tiles, bias):
            tiles = [tiles[c * BLOCK : (c + 1) * BLOCK] for c in range(WINDOW_BLOCKS)]
            return [jnp.where(lower, tiles[-1], tiles[0] + bias)] + tiles[1:-1]

        def unfold(tiles):
            low = [tile.astype(BF16) for tile in tiles]
            return jnp.concatenate([low[0] * far[...]] + low[1:] + [low[0] * near[...]], axis=0)

        def softmax(scores, dweights):
            parts = fold(scores, biases[0])
            dparts = fold(dweights, 0.0)
            shifts = [0.0] + biases[1:-1]
            top = None
            for part, shift in zip(parts, shifts):
                here = jnp.max(part, axis=0, keepdims=True) + shift
                top = here if top is None else jnp.maximum(top, here)
            top = top * SCALE_LOG2
            expo = [
                jnp.exp2(part * SCALE_LOG2 - (top - shift)) for part, shift in zip(parts, shifts)
            ]
            inverse = 1.0 / sum(jnp.sum(e, axis=0, keepdims=True) for e in expo)
            weights = [e * inverse for e in expo]
            delta = sum(
                jnp.sum(w * d, axis=0, keepdims=True) for w, d in zip(weights, dparts)
            )
            dscores = [w * (d - delta) for w, d in zip(weights, dparts)]
            return unfold(weights), unfold(dscores)

        def products_out(g, h, queries, grads, weights_low, dscores_low):
            gc = cols(g)
            out_t = dot(v_t[gc, window], weights_low, 1, 0)
            dquery_t = dot(k_t[gc, window], dscores_low, 1, 0)
            dv[window, gc] += dot(weights_low, grads, 1, 0)
            dk[window, gc] += dot(dscores_low, queries, 1, 0)
            product = None
            for n in range(PAIR):
                hc = cols(h + n)
                att[rows, hc] = out_t[:, cols(n)].T.astype(BF16)
                dquery = dquery_t[:, cols(n)].T * SCALE
                onto = dquery * (q_raw[rows, hc].astype(F32) * scale)
                q_acc[:, hc] += eight(onto)
                gain = q_gain[:, hc]
                u_all[rows, hc] = dquery * gain
                product = onto * gain if product is None else product + onto * gain
            return product

        units = [(h // GROUP, h) for h in range(0, HEADS, PAIR)]
        product = None
        ahead = products_in(*units[0])
        for n, unit in enumerate(units):
            queries, grads, scores, dweights = ahead
            if n + 1 < len(units):
                ahead = products_in(*units[n + 1])
            low = softmax(scores, dweights)
            part = products_out(*unit, queries, grads, *low)
            product = part if product is None else product + part
        return product

    def back_copies(b):
        rows = block_rows(b)
        return [
            remote(back_k.at[rows], got_k.at[rows], back_send.at[0, b], back_recv.at[0, b], ctx=prv),
            remote(back_v.at[rows], got_v.at[rows], back_send.at[1, b], back_recv.at[1, b], ctx=prv),
        ]

    def send_back(b, start=True):
        rows = block_rows(b)
        scale = k_col[rows]
        product = None
        for t in range(GROUPS):
            dkey = dk[rows, cols(t)] * SCALE
            onto = dkey * (k_raw[rows, cols(t)].astype(F32) * scale)
            k_acc[:, cols(t)] += eight(onto)
            back_k[rows, cols(t)] = dkey.astype(BF16)
            back_v[rows, cols(t)] = dv[rows, cols(t)].astype(BF16)
            gain = k_gain[:, cols(t)]
            product = onto * gain if product is None else product + onto * gain
        if start:
            for copy in back_copies(b):
                copy.start()
        hin[pl.ds(b, 1), :] = row_sums(product)

    def exchange(src, dst, send, recv):
        return [
            remote(src, dst.at[head], send.at[r - 1], recv.at[r - 1], head=at_head(r))
            for r in range(1, 4)
        ]

    hin_copies = exchange(hin, hin_all, hin_send, hin_recv)

    def norm_queries(b, slot):
        rows = block_rows(b)
        scale = q_col[rows]
        for t in range(HEADS):
            unit = q_raw[rows, cols(t)].astype(F32) * scale
            qn[slot, :, cols(t)] = (unit * q_gain[:, cols(t)]).astype(BF16)

    def take_halo(n):
        for copy in halo_copies(n):
            copy.wait_recv()
        halo_scale = lax.rsqrt(halo_stat[...] / (KEY_VALUE_HEADS * HEAD_SIZE) + EPS)
        norm_keys(n, halo_scale[n + HALO_BLOCKS : n + HALO_BLOCKS + 1])
        turn_values(n, 0)

    def work(s):
        b = order(s)
        here = ctx * BLOCKS_HERE + b
        doc = docs[here]
        biases = []
        for c in range(WINDOW_BLOCKS):
            there = here - HALO_BLOCKS + c
            same = (docs[jnp.maximum(there, 0)] == doc) & (there >= 0)
            biases.append(jnp.where(same, 0.0, NEGATIVE))
        product = attend(b, biases, qn.at[s % 2])
        norm_queries(order(s + 1), (s + 1) % 2)
        tile = jnp.broadcast_to(row_sums(product), (8, 128))
        inner[b] = tile
        inner_all[head, b] = tile
        for copy in inner_copies(b):
            copy.start()

    def early(s, _):
        @pl.when(s == 3)
        def _():
            relay.wait_recv()
            take_halo(3)

        work(s)
        return 0

    def late(s, _):
        finish_queries(order(s - 4))
        work(s)

        @pl.when(s < 7)
        def _():
            send_back(s - 4)

        @pl.when(s == 6)
        def _():
            send_back(3, start=False)
            hin_all[head] = hin[...]
            for copy in hin_copies:
                copy.start()

        return 0

    hin[...] = jnp.zeros_like(hin)
    norm_queries(order(0), 0)
    lax.fori_loop(0, 4, early, 0)
    for n in range(3):
        take_halo(n)
    lax.fori_loop(4, BLOCKS_HERE, late, 0)

    for b in range(BLOCKS_HERE):
        rows = slice(HALO + b * BLOCK, HALO + (b + 1) * BLOCK)
        scale = k_col[rows]
        product = None
        for t in range(GROUPS):
            onto = dk[rows, cols(t)] * SCALE * (k_raw[rows, cols(t)].astype(F32) * scale)
            k_acc[:, cols(t)] += eight(onto)
            gain = k_gain[:, cols(t)]
            product = onto * gain if product is None else product + onto * gain
        products[b] = product

    for t in range(HEADS):
        gains[t : t + 1] = jnp.sum(q_acc[:, cols(t)], axis=0, keepdims=True)
    for t in range(GROUPS):
        gains[HEADS + t : HEADS + t + 1] = jnp.sum(k_acc[:, cols(t)], axis=0, keepdims=True)
    gains[HEADS + GROUPS :] = jnp.zeros((GAIN_ROWS - HEADS - GROUPS, 128), F32)
    x_copies = [
        remote(gains, gains_x.at[x], gain_send.at[r - 1], gain_recv.at[r - 1], ctx=at_x(r))
        for r in range(1, 4)
    ]
    for copy in x_copies:
        copy.start()
    gains_x[x] = gains[...]
    for b in range(BLOCKS_HERE):
        kin[b : b + 1] = row_sums(products[b])
    kin_copies = exchange(kin, kin_all, kin_send, kin_recv)
    for copy in kin_copies:
        copy.start()
    kin_all[head] = kin[...]

    last_k, last_v = back_copies(HALO_BLOCKS - 1)
    last_k.start()
    for copy in x_copies:
        copy.wait_recv()
    gains_zy[zy] = gains_x[0] + gains_x[1] + gains_x[2] + gains_x[3]
    zy_copies = [
        remote(
            gains_zy.at[zy], gains_zy.at[zy], gain_send.at[r + 2], gain_recv.at[r + 2], ctx=at_zy(r)
        )
        for r in range(1, 8)
    ]
    for copy in zy_copies:
        copy.start()
    for copy in hin_copies:
        copy.wait_recv()
    hin_sum[...] = hin_all[0] + hin_all[1] + hin_all[2] + hin_all[3]
    hin_back = remote(hin_sum, hin_got, hin_send.at[3], hin_recv.at[3], ctx=prv)
    hin_back.start()
    last_v.start()

    def finish_later(s, _):
        finish_queries(order(s))
        return 0

    lax.fori_loop(4, BLOCKS_HERE, finish_later, 0)

    for n in range(HALO_BLOCKS):
        for copy in back_copies(n):
            copy.wait_recv()
    split = TOKENS - HALO
    vgrad[0:split] = dv[HALO : HALO + split].astype(BF16)
    vgrad[split:] = (dv[HALO + split :] + got_v[...].astype(F32)).astype(BF16)

    for copy in kin_copies:
        copy.wait_recv()
    hin_back.wait_recv()
    kin_total = kin_all[0] + kin_all[1] + kin_all[2] + kin_all[3]
    got_total = hin_got[...]
    for b in range(BLOCKS_HERE):
        there = slice(b * BLOCK, (b + 1) * BLOCK)
        rows = slice(HALO + b * BLOCK, HALO + (b + 1) * BLOCK)
        row = kin_total[b : b + 1]
        n = b - (BLOCKS_HERE - HALO_BLOCKS)
        if n >= 0:
            row = row + got_total[n : n + 1]
        mean = column(row / (KEY_VALUE_HEADS * HEAD_SIZE))
        scale = k_col[rows]
        for t in range(GROUPS):
            dkey = dk[rows, cols(t)] * SCALE
            if n >= 0:
                dkey = dkey + got_k[n * BLOCK : (n + 1) * BLOCK, cols(t)].astype(F32)
            unit = k_raw[rows, cols(t)].astype(F32) * scale
            grad = scale * (dkey * k_gain[:, cols(t)] - unit * mean)
            kgrad[there, cols(t)] = grad.astype(BF16)

    for copy in zy_copies:
        copy.wait_recv()
    summed = gains_zy[0]
    for n in range(1, 8):
        summed = summed + gains_zy[n]
    for t in range(HEADS):
        qgain_out[:, cols(t)] = summed[t : t + 1]
    for t in range(GROUPS):
        kgain_out[:, cols(t)] = summed[HEADS + t : HEADS + t + 1]

    for copy in (
        [relay] + stat_copies + hin_copies + [hin_back] + kin_copies + x_copies + zy_copies
    ):
        copy.wait_send()
    for n in range(HALO_BLOCKS):
        for copy in halo_copies(n) + back_copies(n):
            copy.wait_send()

    def drain(b, _):
        for copy in inner_copies(b):
            copy.wait_send()
        return 0

    lax.fori_loop(0, BLOCKS_HERE, drain, 0)


def write(*refs):
    *pairs, sem = refs
    half = len(pairs) // 2
    copies = [
        pltpu.make_async_copy(src, dst, sem.at[n])
        for n, (src, dst) in enumerate(zip(pairs[:half], pairs[half:]))
    ]
    for copy in copies:
        copy.start()
    for copy in copies:
        copy.wait()


def local(query_raw, key_raw, values, output_gradient, query_gain, key_norm_gain, block_docs):
    hbm = pl.BlockSpec(memory_space=pltpu.HBM)
    vmem = pl.BlockSpec(memory_space=pltpu.VMEM)
    sems = pltpu.SemaphoreType.DMA
    stat = pltpu.VMEM((8, 128), F32)
    stats = pltpu.VMEM((HEAD_PEERS, 8, 128), F32)
    gain = pltpu.VMEM((GAIN_ROWS, 128), F32)
    scratch = [
        pltpu.VMEM((1, QCOLS), F32),
        pltpu.VMEM((1, KCOLS), F32),
        pltpu.SMEM((256,), jnp.int32),
        pltpu.VMEM((TOKENS, QCOLS), BF16),
        pltpu.VMEM((TOKENS, QCOLS), BF16),
        pltpu.VMEM((TOKENS, QCOLS), F32),
        pltpu.VMEM((2, BLOCK, QCOLS), BF16),
        pltpu.VMEM((EXT, KCOLS), BF16),
        pltpu.VMEM((EXT, KCOLS), BF16),
        pltpu.VMEM((EXT, KCOLS), BF16),
        pltpu.VMEM((KCOLS, EXT), BF16),
        pltpu.VMEM((KCOLS, EXT), BF16),
        pltpu.VMEM((EXT, KCOLS), F32),
        pltpu.VMEM((EXT, KCOLS), F32),
        pltpu.VMEM((HALO, KCOLS), BF16),
        pltpu.VMEM((HALO, KCOLS), BF16),
        pltpu.VMEM((HALO, KCOLS), BF16),
        pltpu.VMEM((HALO, KCOLS), BF16),
        pltpu.VMEM((TOKENS, 128), F32),
        pltpu.VMEM((EXT, 128), F32),
        pltpu.VMEM((BLOCK, PAIR * BLOCK), F32),
        pltpu.VMEM((BLOCK, PAIR * BLOCK), BF16),
        pltpu.VMEM((BLOCK, PAIR * BLOCK), BF16),
        pltpu.VMEM((16, 128), F32),
        pltpu.VMEM((HEAD_PEERS, 16, 128), F32),
        stat,
        stat,
        pltpu.VMEM((BLOCKS_HERE, 8, 128), F32),
        pltpu.VMEM((HEAD_PEERS, BLOCKS_HERE, 8, 128), F32),
        stat,
        stats,
        stat,
        stats,
        stat,
        stat,
        pltpu.VMEM((8, QCOLS), F32),
        pltpu.VMEM((8, KCOLS), F32),
        pltpu.VMEM((BLOCKS_HERE, 128, 128), F32),
        gain,
        pltpu.VMEM((4, GAIN_ROWS, 128), F32),
        pltpu.VMEM((8, GAIN_ROWS, 128), F32),
        sems((6 + QUERY_PIECES,)),
        sems((9,)),
        sems((9,)),
        sems((3,)),
        sems((3,)),
        sems((3, BLOCKS_HERE)),
        sems((3, BLOCKS_HERE)),
        sems((2, HALO_BLOCKS)),
        sems((2, HALO_BLOCKS)),
        sems((3,)),
        sems((3,)),
        sems((4,)),
        sems((4,)),
        sems((10,)),
        sems((10,)),
    ]
    shapes = [
        ((TOKENS, QCOLS), BF16),
        ((TOKENS, QCOLS), BF16),
        ((TOKENS, KCOLS), BF16),
        ((TOKENS, KCOLS), BF16),
        ((1, QCOLS), F32),
        ((1, KCOLS), F32),
    ]
    held = pl.pallas_call(
        kernel,
        out_shape=[pltpu.VMEM(*shape) for shape in shapes],
        in_specs=[hbm] * 7,
        out_specs=[vmem] * 6,
        scratch_shapes=scratch,
        compiler_params=pltpu.CompilerParams(
            collective_id=0, has_side_effects=True, vmem_limit_bytes=56 * 2**20
        ),
        cost_estimate=pl.CostEstimate(
            flops=8_000_000_000, bytes_accessed=10_000_000, transcendentals=5_000_000
        ),
    )(
        query_raw, key_raw, values, output_gradient,
        query_gain.reshape(1, QCOLS), key_norm_gain.reshape(1, KCOLS), block_docs,
    )
    outs = pl.pallas_call(
        write,
        out_shape=[jax.ShapeDtypeStruct(*shape) for shape in shapes],
        in_specs=[vmem] * 6,
        out_specs=[hbm] * 6,
        scratch_shapes=[sems((6,))],
        compiler_params=pltpu.CompilerParams(vmem_limit_bytes=16 * 2**20),
    )(*[pltpu.with_memory_space_constraint(x, pltpu.VMEM) for x in held])
    return (*outs[:4], outs[4].reshape(QCOLS), outs[5].reshape(KCOLS))


def solution(mesh):
    placed = (
        P("ctx", "head"),
        P("ctx", "head"),
        P("ctx", "head"),
        P("ctx", "head"),
        P("head"),
        P("head"),
        P(),
    )
    return jax.shard_map(
        local,
        mesh=mesh,
        in_specs=placed,
        out_specs=(
            P("ctx", "head"),
            P("ctx", "head"),
            P("ctx", "head"),
            P("ctx", "head"),
            P("head"),
            P("head"),
        ),
        check_vma=False,
    )
```

```python
import jax
import jax.numpy as jnp
from jax import lax
from jax.experimental import pallas as pl
from jax.experimental.pallas import tpu as pltpu
from jax.sharding import PartitionSpec as P

QUERY_HEADS = 32
KEY_VALUE_HEADS = 8
HEAD_SIZE = 128
WINDOW_REACH = 512
BLOCK = 128
EPS = 1e-06
NEGATIVE = -1e30
SCALE = HEAD_SIZE ** (-0.5)
SCALE_LOG2 = SCALE * 1.4426950408889634

F32 = jnp.float32
BF16 = jnp.bfloat16
MESH = pl.DeviceIdType.MESH

TOKENS = 1024
BLOCKS_HERE = TOKENS // BLOCK
HALO = WINDOW_REACH
HALO_BLOCKS = HALO // BLOCK
WINDOW_BLOCKS = HALO_BLOCKS + 1
WINDOW = WINDOW_BLOCKS * BLOCK
EXT = HALO + TOKENS
GROUPS = 2
GROUP = 4
PAIR = 2
QUERY_PIECES = 4
HEADS = GROUPS * GROUP
QCOLS = HEADS * HEAD_SIZE
KCOLS = GROUPS * HEAD_SIZE
HEAD_PEERS = 4
GAIN_ROWS = 16


def dot(a, b, ca, cb):
    return lax.dot_general(a, b, (((ca,), (cb,)), ((), ())), preferred_element_type=F32)


def block_rows(b):
    return pl.ds(pl.multiple_of(b * BLOCK, BLOCK), BLOCK)


def cols(t):
    return slice(t * 128, (t + 1) * 128)


def column(row):
    return jnp.broadcast_to(row, (128, 128)).T


def row_sums(tile):
    return jnp.sum(tile.T, axis=0, keepdims=True)


def eight(tile):
    return jnp.sum(tile.reshape(16, 8, tile.shape[1]), axis=0)


def kernel(
    q_in, k_in, v_in, g_in, q_gain_in, k_gain_in, docs_in,
    att, qgrad, kgrad, vgrad, qgain_out, kgain_out,
    q_gain, k_gain, docs,
    q_raw, go, u_all, qn,
    k_raw, vals, kn, k_t, v_t, dk, dv,
    back_k, back_v, got_k, got_v,
    q_col, k_col, tri, near, far,
    stat, stat_all, k_stat, halo_stat,
    inner, inner_all, kin, kin_all, hin, hin_all, hin_sum, hin_got,
    q_acc, k_acc, products, gains, gains_x, gains_zy,
    load_sem, halo_send, halo_recv, stat_send, stat_recv,
    inner_send, inner_recv, back_send, back_recv, kin_send, kin_recv,
    hin_send, hin_recv, gain_send, gain_recv,
):
    ctx = lax.axis_index("ctx")
    head = lax.axis_index("head")
    x = ctx % 4
    z = (ctx // 4) % 4
    y = ctx // 16
    nxt = (ctx + 1) % 32
    prv = (ctx + 31) % 32

    def at_x(r):
        return (y * 4 + z) * 4 + (x + r) % 4

    zy = y * 4 + z

    def at_zy(r):
        return ((zy + r) % 8) * 4 + x

    def at_head(r):
        return (head + r) % HEAD_PEERS

    def remote(src, dst, send, recv, **where):
        return pltpu.make_async_remote_copy(
            src_ref=src, dst_ref=dst, send_sem=send, recv_sem=recv,
            device_id=where, device_id_type=MESH,
        )

    own = pl.ds(HALO, TOKENS)
    load_k = pltpu.make_async_copy(k_in, k_raw.at[own], load_sem.at[0])
    load_v = pltpu.make_async_copy(v_in, vals.at[own], load_sem.at[1])
    load_g = pltpu.make_async_copy(g_in, go, load_sem.at[2])
    load_q = []
    for n in range(QUERY_PIECES):
        rows = pl.ds(n * (TOKENS // QUERY_PIECES), TOKENS // QUERY_PIECES)
        load_q.append(pltpu.make_async_copy(q_in.at[rows], q_raw.at[rows], load_sem.at[3 + n]))
    for copy in load_q:
        copy.start()
    load_k.start()
    load_small = [
        pltpu.make_async_copy(q_gain_in, q_gain, load_sem.at[3 + QUERY_PIECES]),
        pltpu.make_async_copy(k_gain_in, k_gain, load_sem.at[4 + QUERY_PIECES]),
        pltpu.make_async_copy(docs_in, docs, load_sem.at[5 + QUERY_PIECES]),
    ]
    for copy in load_small:
        copy.start()

    barrier = pltpu.get_barrier_semaphore()
    for r in range(1, 4):
        pl.semaphore_signal(barrier, inc=1, device_id={"head": at_head(r)}, device_id_type=MESH)
        pl.semaphore_signal(barrier, inc=1, device_id={"ctx": at_x(r)}, device_id_type=MESH)
    for r in range(1, 8):
        pl.semaphore_signal(barrier, inc=1, device_id={"ctx": at_zy(r)}, device_id_type=MESH)
    for other in (nxt, prv):
        pl.semaphore_signal(barrier, inc=1, device_id={"ctx": other}, device_id_type=MESH)

    def halo_copies(n):
        there = pl.ds(TOKENS - HALO + n * BLOCK, BLOCK)
        here = pl.ds(n * BLOCK, BLOCK)
        return [
            remote(k_in.at[there], k_raw.at[here], halo_send.at[n], halo_recv.at[n], ctx=nxt),
            remote(
                v_in.at[there], vals.at[here], halo_send.at[4 + n], halo_recv.at[4 + n], ctx=nxt
            ),
        ]

    def send_halo(*chunks):
        for n in chunks:
            for copy in halo_copies(n):
                copy.start()

    for b in range(BLOCKS_HERE):
        if b % (BLOCKS_HERE // QUERY_PIECES) == 0:
            load_q[b * QUERY_PIECES // BLOCKS_HERE].wait()
        rows = slice(b * BLOCK, (b + 1) * BLOCK)
        total = None
        for t in range(HEADS):
            part = q_raw[rows, cols(t)].astype(F32)
            total = part * part if total is None else total + part * part
        stat[b : b + 1] = row_sums(total)
    load_k.wait()
    load_v.start()
    load_g.start()
    for b in range(BLOCKS_HERE):
        rows = slice(HALO + b * BLOCK, HALO + (b + 1) * BLOCK)
        total = None
        for t in range(GROUPS):
            part = k_raw[rows, cols(t)].astype(F32)
            total = part * part if total is None else total + part * part
        stat[b + 8 : b + 9] = row_sums(total)

    pl.semaphore_wait(barrier, 15)
    stat_copies = [
        remote(stat, stat_all.at[head], stat_send.at[r - 1], stat_recv.at[r - 1], head=at_head(r))
        for r in range(1, 4)
    ]
    for copy in stat_copies:
        copy.start()
    stat_all[head] = stat[...]

    send_halo(3)

    key_at = lax.broadcasted_iota(jnp.int32, (BLOCK, BLOCK), 0)
    query_at = lax.broadcasted_iota(jnp.int32, (BLOCK, BLOCK), 1)
    lower = jnp.where(key_at <= query_at, 1.0, 0.0)
    tri[...] = jnp.concatenate([lower] * PAIR, axis=1)
    near[...] = jnp.concatenate([lower] * PAIR, axis=1).astype(BF16)
    far[...] = (1.0 - jnp.concatenate([lower] * PAIR, axis=1)).astype(BF16)
    dk[...] = jnp.zeros_like(dk)
    dv[...] = jnp.zeros_like(dv)
    q_acc[...] = jnp.zeros_like(q_acc)
    k_acc[...] = jnp.zeros_like(k_acc)
    load_v.wait()

    def turn_values(b, _):
        rows = block_rows(b)
        for t in range(GROUPS):
            v_t[cols(t), rows] = vals[rows, cols(t)].T
        return 0

    lax.fori_loop(HALO_BLOCKS, EXT // BLOCK, turn_values, 0)

    for copy in stat_copies:
        copy.wait_recv()
    total = stat_all[0] + stat_all[1] + stat_all[2] + stat_all[3]
    k_stat[...] = total[8:16]
    relay = remote(k_stat, halo_stat, halo_send.at[8], halo_recv.at[8], ctx=nxt)
    relay.start()
    send_halo(2, 1, 0)

    q_scale = lax.rsqrt(total[0:8] / (QUERY_HEADS * HEAD_SIZE) + EPS)
    for b in range(BLOCKS_HERE):
        q_col[b * BLOCK : (b + 1) * BLOCK] = column(q_scale[b : b + 1])

    def norm_keys(b, scale_row):
        rows = slice(b * BLOCK, (b + 1) * BLOCK)
        scale = column(scale_row)
        k_col[rows] = scale
        for t in range(GROUPS):
            unit = k_raw[rows, cols(t)].astype(F32) * scale
            normed = (unit * k_gain[:, cols(t)]).astype(BF16)
            kn[rows, cols(t)] = normed
            k_t[cols(t), rows] = normed.T

    for copy in load_small:
        copy.wait()
    k_scale = lax.rsqrt(total[8:16] / (KEY_VALUE_HEADS * HEAD_SIZE) + EPS)
    for b in range(BLOCKS_HERE):
        norm_keys(b + HALO_BLOCKS, k_scale[b : b + 1])
    load_g.wait()

    def order(s):
        return jnp.where(s < 3, s + 4, jnp.where(s == 3, 3, jnp.where(s < 7, s - 4, 7)))

    def inner_copies(b):
        return [
            remote(
                inner.at[b], inner_all.at[head, b],
                inner_send.at[r - 1, b], inner_recv.at[r - 1, b], head=at_head(r),
            )
            for r in range(1, 4)
        ]

    def finish_queries(b):
        rows = block_rows(b)
        for copy in inner_copies(b):
            copy.wait_recv()
        summed = inner_all[0, b] + inner_all[1, b] + inner_all[2, b] + inner_all[3, b]
        mean = column(summed[0:1] / (QUERY_HEADS * HEAD_SIZE))
        scale = q_col[rows]
        for t in range(HEADS):
            unit = q_raw[rows, cols(t)].astype(F32) * scale
            qgrad[rows, cols(t)] = (scale * (u_all[rows, cols(t)] - unit * mean)).astype(BF16)

    def attend(b, biases, qn):
        rows = block_rows(b)
        window = pl.ds(pl.multiple_of(b * BLOCK, BLOCK), WINDOW)
        lower = tri[...] > 0.5
        scale = q_col[rows]

        def products_in(g, h):
            queries = jnp.concatenate([qn[:, cols(h + n)] for n in range(PAIR)], axis=0)
            grads = jnp.concatenate([go[rows, cols(h + n)] for n in range(PAIR)], axis=0)
            scores = dot(kn[window, cols(g)], queries, 1, 1)
            dweights = dot(vals[window, cols(g)], grads, 1, 1)
            return queries, grads, scores, dweights

        def fold(tiles, bias):
            tiles = [tiles[c * BLOCK : (c + 1) * BLOCK] for c in range(WINDOW_BLOCKS)]
            return [jnp.where(lower, tiles[-1], tiles[0] + bias)] + tiles[1:-1]

        def unfold(tiles):
            low = [tile.astype(BF16) for tile in tiles]
            return jnp.concatenate([low[0] * far[...]] + low[1:] + [low[0] * near[...]], axis=0)

        def softmax(scores, dweights):
            parts = fold(scores, biases[0])
            dparts = fold(dweights, 0.0)
            shifts = [0.0] + biases[1:-1]
            top = None
            for part, shift in zip(parts, shifts):
                here = jnp.max(part, axis=0, keepdims=True) + shift
                top = here if top is None else jnp.maximum(top, here)
            top = top * SCALE_LOG2
            expo = [
                jnp.exp2(part * SCALE_LOG2 - (top - shift)) for part, shift in zip(parts, shifts)
            ]
            inverse = 1.0 / sum(jnp.sum(e, axis=0, keepdims=True) for e in expo)
            weights = [e * inverse for e in expo]
            delta = sum(
                jnp.sum(w * d, axis=0, keepdims=True) for w, d in zip(weights, dparts)
            )
            dscores = [w * (d - delta) for w, d in zip(weights, dparts)]
            return unfold(weights), unfold(dscores)

        def products_out(g, h, queries, grads, weights_low, dscores_low):
            gc = cols(g)
            out_t = dot(v_t[gc, window], weights_low, 1, 0)
            dquery_t = dot(k_t[gc, window], dscores_low, 1, 0)
            dv[window, gc] += dot(weights_low, grads, 1, 0)
            dk[window, gc] += dot(dscores_low, queries, 1, 0)
            product = None
            for n in range(PAIR):
                hc = cols(h + n)
                att[rows, hc] = out_t[:, cols(n)].T.astype(BF16)
                dquery = dquery_t[:, cols(n)].T * SCALE
                onto = dquery * (q_raw[rows, hc].astype(F32) * scale)
                q_acc[:, hc] += eight(onto)
                gain = q_gain[:, hc]
                u_all[rows, hc] = dquery * gain
                product = onto * gain if product is None else product + onto * gain
            return product

        units = [(h // GROUP, h) for h in range(0, HEADS, PAIR)]
        product = None
        ahead = products_in(*units[0])
        for n, unit in enumerate(units):
            queries, grads, scores, dweights = ahead
            if n + 1 < len(units):
                ahead = products_in(*units[n + 1])
            low = softmax(scores, dweights)
            part = products_out(*unit, queries, grads, *low)
            product = part if product is None else product + part
        return product

    def back_copies(b):
        rows = block_rows(b)
        return [
            remote(back_k.at[rows], got_k.at[rows], back_send.at[0, b], back_recv.at[0, b], ctx=prv),
            remote(back_v.at[rows], got_v.at[rows], back_send.at[1, b], back_recv.at[1, b], ctx=prv),
        ]

    def send_back(b, start=True):
        rows = block_rows(b)
        scale = k_col[rows]
        product = None
        for t in range(GROUPS):
            dkey = dk[rows, cols(t)] * SCALE
            onto = dkey * (k_raw[rows, cols(t)].astype(F32) * scale)
            k_acc[:, cols(t)] += eight(onto)
            back_k[rows, cols(t)] = dkey.astype(BF16)
            back_v[rows, cols(t)] = dv[rows, cols(t)].astype(BF16)
            gain = k_gain[:, cols(t)]
            product = onto * gain if product is None else product + onto * gain
        if start:
            for copy in back_copies(b):
                copy.start()
        hin[pl.ds(b, 1), :] = row_sums(product)

    def exchange(src, dst, send, recv):
        return [
            remote(src, dst.at[head], send.at[r - 1], recv.at[r - 1], head=at_head(r))
            for r in range(1, 4)
        ]

    hin_copies = exchange(hin, hin_all, hin_send, hin_recv)

    def norm_queries(b, slot):
        rows = block_rows(b)
        scale = q_col[rows]
        for t in range(HEADS):
            unit = q_raw[rows, cols(t)].astype(F32) * scale
            qn[slot, :, cols(t)] = (unit * q_gain[:, cols(t)]).astype(BF16)

    def take_halo(n):
        for copy in halo_copies(n):
            copy.wait_recv()
        halo_scale = lax.rsqrt(halo_stat[...] / (KEY_VALUE_HEADS * HEAD_SIZE) + EPS)
        norm_keys(n, halo_scale[n + HALO_BLOCKS : n + HALO_BLOCKS + 1])
        turn_values(n, 0)

    def work(s):
        b = order(s)
        here = ctx * BLOCKS_HERE + b
        doc = docs[here]
        biases = []
        for c in range(WINDOW_BLOCKS):
            there = here - HALO_BLOCKS + c
            same = (docs[jnp.maximum(there, 0)] == doc) & (there >= 0)
            biases.append(jnp.where(same, 0.0, NEGATIVE))
        product = attend(b, biases, qn.at[s % 2])
        norm_queries(order(s + 1), (s + 1) % 2)
        tile = jnp.broadcast_to(row_sums(product), (8, 128))
        inner[b] = tile
        inner_all[head, b] = tile
        for copy in inner_copies(b):
            copy.start()

    def early(s, _):
        @pl.when(s == 3)
        def _():
            relay.wait_recv()
            take_halo(3)

        work(s)
        return 0

    def late(s, _):
        finish_queries(order(s - 4))
        work(s)

        @pl.when(s < 7)
        def _():
            send_back(s - 4)

        @pl.when(s == 6)
        def _():
            send_back(3, start=False)
            hin_all[head] = hin[...]
            for copy in hin_copies:
                copy.start()

        return 0

    hin[...] = jnp.zeros_like(hin)
    norm_queries(order(0), 0)
    lax.fori_loop(0, 4, early, 0)
    for n in range(3):
        take_halo(n)
    lax.fori_loop(4, BLOCKS_HERE, late, 0)

    def x_phase(part):
        rows = pl.ds(part * HEADS, HEADS)
        return [
            remote(
                gains.at[rows], gains_x.at[x, rows],
                gain_send.at[r - 1 + 10 * part], gain_recv.at[r - 1 + 10 * part], ctx=at_x(r),
            )
            for r in range(1, 4)
        ]

    for t in range(HEADS):
        gains[t : t + 1] = jnp.sum(q_acc[:, cols(t)], axis=0, keepdims=True)
    x_copies = x_phase(0)
    for copy in x_copies:
        copy.start()
    gains_x[x, 0:HEADS] = gains[0:HEADS]

    for b in range(BLOCKS_HERE):
        rows = slice(HALO + b * BLOCK, HALO + (b + 1) * BLOCK)
        scale = k_col[rows]
        product = None
        for t in range(GROUPS):
            onto = dk[rows, cols(t)] * SCALE * (k_raw[rows, cols(t)].astype(F32) * scale)
            k_acc[:, cols(t)] += eight(onto)
            gain = k_gain[:, cols(t)]
            product = onto * gain if product is None else product + onto * gain
        products[b] = product

    for t in range(GROUPS):
        gains[HEADS + t : HEADS + t + 1] = jnp.sum(k_acc[:, cols(t)], axis=0, keepdims=True)
    gains[HEADS + GROUPS :] = jnp.zeros((GAIN_ROWS - HEADS - GROUPS, 128), F32)
    key_copies = x_phase(1)
    for copy in key_copies:
        copy.start()
    gains_x[x, HEADS:] = gains[HEADS:]
    x_copies = x_copies + key_copies
    for b in range(BLOCKS_HERE):
        kin[b : b + 1] = row_sums(products[b])
    kin_copies = exchange(kin, kin_all, kin_send, kin_recv)
    for copy in kin_copies:
        copy.start()
    kin_all[head] = kin[...]

    last_k, last_v = back_copies(HALO_BLOCKS - 1)
    last_k.start()
    for copy in x_copies:
        copy.wait_recv()
    gains_zy[zy] = gains_x[0] + gains_x[1] + gains_x[2] + gains_x[3]
    zy_copies = [
        remote(
            gains_zy.at[zy], gains_zy.at[zy], gain_send.at[r + 2], gain_recv.at[r + 2], ctx=at_zy(r)
        )
        for r in range(1, 8)
    ]
    for copy in zy_copies:
        copy.start()
    for copy in hin_copies:
        copy.wait_recv()
    hin_sum[...] = hin_all[0] + hin_all[1] + hin_all[2] + hin_all[3]
    hin_back = remote(hin_sum, hin_got, hin_send.at[3], hin_recv.at[3], ctx=prv)
    hin_back.start()
    last_v.start()

    def finish_later(s, _):
        finish_queries(order(s))
        return 0

    lax.fori_loop(4, BLOCKS_HERE, finish_later, 0)

    for n in range(HALO_BLOCKS):
        for copy in back_copies(n):
            copy.wait_recv()
    split = TOKENS - HALO
    vgrad[0:split] = dv[HALO : HALO + split].astype(BF16)
    vgrad[split:] = (dv[HALO + split :] + got_v[...].astype(F32)).astype(BF16)

    for copy in kin_copies:
        copy.wait_recv()
    hin_back.wait_recv()
    kin_total = kin_all[0] + kin_all[1] + kin_all[2] + kin_all[3]
    got_total = hin_got[...]
    for b in range(BLOCKS_HERE):
        there = slice(b * BLOCK, (b + 1) * BLOCK)
        rows = slice(HALO + b * BLOCK, HALO + (b + 1) * BLOCK)
        row = kin_total[b : b + 1]
        n = b - (BLOCKS_HERE - HALO_BLOCKS)
        if n >= 0:
            row = row + got_total[n : n + 1]
        mean = column(row / (KEY_VALUE_HEADS * HEAD_SIZE))
        scale = k_col[rows]
        for t in range(GROUPS):
            dkey = dk[rows, cols(t)] * SCALE
            if n >= 0:
                dkey = dkey + got_k[n * BLOCK : (n + 1) * BLOCK, cols(t)].astype(F32)
            unit = k_raw[rows, cols(t)].astype(F32) * scale
            grad = scale * (dkey * k_gain[:, cols(t)] - unit * mean)
            kgrad[there, cols(t)] = grad.astype(BF16)

    for copy in zy_copies:
        copy.wait_recv()
    summed = gains_zy[0]
    for n in range(1, 8):
        summed = summed + gains_zy[n]
    for t in range(HEADS):
        qgain_out[:, cols(t)] = summed[t : t + 1]
    for t in range(GROUPS):
        kgain_out[:, cols(t)] = summed[HEADS + t : HEADS + t + 1]

    for copy in (
        [relay] + stat_copies + hin_copies + [hin_back] + kin_copies + x_copies + zy_copies
    ):
        copy.wait_send()
    for n in range(HALO_BLOCKS):
        for copy in halo_copies(n) + back_copies(n):
            copy.wait_send()

    def drain(b, _):
        for copy in inner_copies(b):
            copy.wait_send()
        return 0

    lax.fori_loop(0, BLOCKS_HERE, drain, 0)


def write(*refs):
    *pairs, sem = refs
    half = len(pairs) // 2
    copies = [
        pltpu.make_async_copy(src, dst, sem.at[n])
        for n, (src, dst) in enumerate(zip(pairs[:half], pairs[half:]))
    ]
    for copy in copies:
        copy.start()
    for copy in copies:
        copy.wait()


def local(query_raw, key_raw, values, output_gradient, query_gain, key_norm_gain, block_docs):
    hbm = pl.BlockSpec(memory_space=pltpu.HBM)
    vmem = pl.BlockSpec(memory_space=pltpu.VMEM)
    sems = pltpu.SemaphoreType.DMA
    stat = pltpu.VMEM((8, 128), F32)
    stats = pltpu.VMEM((HEAD_PEERS, 8, 128), F32)
    gain = pltpu.VMEM((GAIN_ROWS, 128), F32)
    scratch = [
        pltpu.VMEM((1, QCOLS), F32),
        pltpu.VMEM((1, KCOLS), F32),
        pltpu.SMEM((256,), jnp.int32),
        pltpu.VMEM((TOKENS, QCOLS), BF16),
        pltpu.VMEM((TOKENS, QCOLS), BF16),
        pltpu.VMEM((TOKENS, QCOLS), F32),
        pltpu.VMEM((2, BLOCK, QCOLS), BF16),
        pltpu.VMEM((EXT, KCOLS), BF16),
        pltpu.VMEM((EXT, KCOLS), BF16),
        pltpu.VMEM((EXT, KCOLS), BF16),
        pltpu.VMEM((KCOLS, EXT), BF16),
        pltpu.VMEM((KCOLS, EXT), BF16),
        pltpu.VMEM((EXT, KCOLS), F32),
        pltpu.VMEM((EXT, KCOLS), F32),
        pltpu.VMEM((HALO, KCOLS), BF16),
        pltpu.VMEM((HALO, KCOLS), BF16),
        pltpu.VMEM((HALO, KCOLS), BF16),
        pltpu.VMEM((HALO, KCOLS), BF16),
        pltpu.VMEM((TOKENS, 128), F32),
        pltpu.VMEM((EXT, 128), F32),
        pltpu.VMEM((BLOCK, PAIR * BLOCK), F32),
        pltpu.VMEM((BLOCK, PAIR * BLOCK), BF16),
        pltpu.VMEM((BLOCK, PAIR * BLOCK), BF16),
        pltpu.VMEM((16, 128), F32),
        pltpu.VMEM((HEAD_PEERS, 16, 128), F32),
        stat,
        stat,
        pltpu.VMEM((BLOCKS_HERE, 8, 128), F32),
        pltpu.VMEM((HEAD_PEERS, BLOCKS_HERE, 8, 128), F32),
        stat,
        stats,
        stat,
        stats,
        stat,
        stat,
        pltpu.VMEM((8, QCOLS), F32),
        pltpu.VMEM((8, KCOLS), F32),
        pltpu.VMEM((BLOCKS_HERE, 128, 128), F32),
        gain,
        pltpu.VMEM((4, GAIN_ROWS, 128), F32),
        pltpu.VMEM((8, GAIN_ROWS, 128), F32),
        sems((6 + QUERY_PIECES,)),
        sems((9,)),
        sems((9,)),
        sems((3,)),
        sems((3,)),
        sems((3, BLOCKS_HERE)),
        sems((3, BLOCKS_HERE)),
        sems((2, HALO_BLOCKS)),
        sems((2, HALO_BLOCKS)),
        sems((3,)),
        sems((3,)),
        sems((4,)),
        sems((4,)),
        sems((13,)),
        sems((13,)),
    ]
    shapes = [
        ((TOKENS, QCOLS), BF16),
        ((TOKENS, QCOLS), BF16),
        ((TOKENS, KCOLS), BF16),
        ((TOKENS, KCOLS), BF16),
        ((1, QCOLS), F32),
        ((1, KCOLS), F32),
    ]
    held = pl.pallas_call(
        kernel,
        out_shape=[pltpu.VMEM(*shape) for shape in shapes],
        in_specs=[hbm] * 7,
        out_specs=[vmem] * 6,
        scratch_shapes=scratch,
        compiler_params=pltpu.CompilerParams(
            collective_id=0, has_side_effects=True, vmem_limit_bytes=56 * 2**20
        ),
        cost_estimate=pl.CostEstimate(
            flops=8_000_000_000, bytes_accessed=10_000_000, transcendentals=5_000_000
        ),
    )(
        query_raw, key_raw, values, output_gradient,
        query_gain.reshape(1, QCOLS), key_norm_gain.reshape(1, KCOLS), block_docs,
    )
    outs = pl.pallas_call(
        write,
        out_shape=[jax.ShapeDtypeStruct(*shape) for shape in shapes],
        in_specs=[vmem] * 6,
        out_specs=[hbm] * 6,
        scratch_shapes=[sems((6,))],
        compiler_params=pltpu.CompilerParams(vmem_limit_bytes=16 * 2**20),
    )(*[pltpu.with_memory_space_constraint(x, pltpu.VMEM) for x in held])
    return (*outs[:4], outs[4].reshape(QCOLS), outs[5].reshape(KCOLS))


def solution(mesh):
    placed = (
        P("ctx", "head"),
        P("ctx", "head"),
        P("ctx", "head"),
        P("ctx", "head"),
        P("head"),
        P("head"),
        P(),
    )
    return jax.shard_map(
        local,
        mesh=mesh,
        in_specs=placed,
        out_specs=(
            P("ctx", "head"),
            P("ctx", "head"),
            P("ctx", "head"),
            P("ctx", "head"),
            P("head"),
            P("head"),
        ),
        check_vma=False,
    )
```
